128 devices in a mesh: row: 8 (over z, y_hi), col: 16 (over y_lo, x, core).
Axes of the slice: x: 4, y: 4 (y_hi: 2, y_lo: 2; y = y_hi * 2 + y_lo), z: 4, core: 2. Of those that a mesh axis runs over, the one named last changes fastest.
Arguments:
- raster: bfloat16 [1024, 1024, 128], P('row', 'col'), may hold values from -6 to 6
- conv_first: bfloat16 [3, 3, 128, 128], replicated, may hold values from -0.1875 to 0.1875
- conv_second: bfloat16 [3, 3, 128, 128], replicated, may hold values from -0.1875 to 0.1875
- crop_anchor: int32 [2, 4096], P(None, ('row', 'col')), may hold values from 0 to 1008, as said below
- agent_live: int32 [4096], P(('row', 'col')), may hold values from 0 to 1, as said below
- w_embed: bfloat16 [2048, 512], replicated, may hold values from -0.125 to 0.125
- gain_attn: float32 [512], replicated, may hold values from 0.25 to 1.75
- w_qkv: bfloat16 [512, 1536], replicated, may hold values from -0.25 to 0.25
- w_out: bfloat16 [512, 512], replicated, may hold values from -0.25 to 0.25
- gain_mlp: float32 [512], replicated, may hold values from 0.25 to 1.75
- w_up: bfloat16 [512, 2048], replicated, may hold values from -0.25 to 0.25
- w_down: bfloat16 [2048, 512], replicated, may hold values from -0.125 to 0.125
Outputs:
- features: bfloat16 [1024, 1024, 128], P('row', 'col')
- agent_out: bfloat16 [4096, 512], P(('row', 'col'))
The draws below stay inside these ranges and needn't reach their ends.
Inputs may be any that keep to these rules, and one draw needn't show every extreme that they name: `crop_anchor`: the block of device (r, o) along row+col holds at column d * 2 + k the top-left cell of the crop for slot o * 2 + k of shard (r, d). That cell lies in grid rows r * 128 to r * 128 + 127 and grid columns o * 64 to o * 64 + 63, and the whole crop lies inside the grid. `agent_live`: every shard (an aligned block of 32 slots) has at least one live slot, and some shard has all 32 live.
All inputs are finite; a program needn't handle non-finite values.
Results may differ from the reference program's by a relative error of at most 0.0095.
Values may be sent and summed in bfloat16 or wider, within the bound.
No kernel may reach another device: no remote copies, remote signals or barrier semaphores. Data moves between devices by JAX's collectives and lax.ppermute only.
A program may use at most 128 MiB of HBM per device.

```python
import jax
import jax.numpy as jnp
from jax import lax

C = 128
D = 512
HEADS = 8
FF = 2048
CROP = 16
POOL = 4
CELL_R = 128
CELL_C = 64
CAP = 2
HEAD_DIM = 64
PATCH_FEAT = 2048
GRID_COLS = 16
H = 1024
W = 1024
SLOTS = 32
AGENT_SLOTS = 4096


def draw_crop_anchor(key, part):
    slot_ids = jnp.arange(AGENT_SLOTS, dtype=jnp.int32)
    shard_ids = slot_ids // SLOTS
    band_ids = shard_ids // GRID_COLS
    owner_ids = shard_ids % GRID_COLS
    row_span = jnp.minimum(CELL_R, H - CROP + 1 - band_ids * CELL_R)
    col_span = jnp.minimum(CELL_C, W - CROP + 1 - owner_ids * CELL_C)
    key_row, key_col = jax.random.split(jax.random.fold_in(key, 11))
    row_offset = jax.random.randint(key_row, (AGENT_SLOTS,), 0, row_span)
    col_offset = jax.random.randint(key_col, (AGENT_SLOTS,), 0, col_span)
    row_offset = jnp.where(slot_ids == 0, 0, row_offset)
    col_offset = jnp.where(slot_ids == 0, 0, col_offset)
    row_offset = jnp.where(slot_ids == AGENT_SLOTS - 1, row_span - 1, row_offset)
    col_offset = jnp.where(slot_ids == AGENT_SLOTS - 1, col_span - 1, col_offset)
    return jnp.stack([band_ids * CELL_R + row_offset, owner_ids * CELL_C + col_offset]).astype(jnp.int32)


def draw_agent_live(key, part):
    key_count, key_full, key_order = jax.random.split(jax.random.fold_in(key, 23), 3)
    shard_total = AGENT_SLOTS // SLOTS
    counts = jax.random.randint(key_count, (shard_total,), 1, SLOTS + 1)
    full_shard = jax.random.randint(key_full, (), 0, shard_total)
    counts = jnp.where(jnp.arange(shard_total) == full_shard, SLOTS, counts)
    ranks = jax.vmap(lambda sub_key: jax.random.permutation(sub_key, SLOTS))(jax.random.split(key_order, shard_total))
    return (ranks < counts[:, None]).astype(jnp.int32).reshape(AGENT_SLOTS)


def block_levels(stream_key, extent, shards, low, largest):
    def one(axis_at, blocks):
        heights = jax.random.uniform(jax.random.fold_in(jax.random.fold_in(stream_key, 6), axis_at), (blocks,), jnp.float32, low / len(shards), largest / len(shards))
        return jnp.repeat(jnp.exp(heights), extent[axis_at] // blocks).reshape((-1,) + (1,) * (len(extent) - axis_at - 1))

    loudness = one(*shards[0])
    for cut in shards[1:]:
        loudness = loudness * one(*cut)
    return loudness


def noise(key, shape, scale, reach, shards=(), held_as=jnp.bfloat16):
    result = jax.random.normal(key, shape, jnp.float32) * scale
    if len(shards) > 0:
        result = block_levels(key, shape, shards, -0.22, 0.18) * result
    return jnp.clip(result, min=-reach, max=reach).astype(held_as)


def setup_inputs(seed: int = 0) -> dict:
    streams_of = jax.random.split(jax.random.key(seed), 13)
    raster = noise(streams_of[0], (H, W, C), 1.0, 6.0, ((0, 8), (1, 16)))
    conv_first = noise(streams_of[1], (3, 3, C, C), (9 * C) ** -0.5, 0.1875)
    conv_second = noise(streams_of[2], (3, 3, C, C), (9 * C) ** -0.5, 0.1875)
    crop_anchor = draw_crop_anchor(jax.random.fold_in(streams_of[12], 71), 0)
    agent_live = draw_agent_live(jax.random.fold_in(streams_of[12], 71), 0)
    w_embed = noise(streams_of[5], (PATCH_FEAT, D), PATCH_FEAT ** -0.5, 0.125)
    gain_attn = jnp.clip(1.0 + 0.15 * jax.random.normal(streams_of[6], (D,), jnp.float32), 0.25, 1.75)
    w_qkv = noise(streams_of[7], (D, 3 * D), D ** -0.5, 0.25)
    w_out = noise(streams_of[8], (D, D), D ** -0.5, 0.25)
    gain_mlp = jnp.clip(1.0 + 0.15 * jax.random.normal(streams_of[9], (D,), jnp.float32), 0.25, 1.75)
    w_up = noise(streams_of[10], (D, FF), D ** -0.5, 0.25)
    w_down = noise(streams_of[11], (FF, D), FF ** -0.5, 0.125)
    return {"raster": raster, "conv_first": conv_first, "conv_second": conv_second, "crop_anchor": crop_anchor, "agent_live": agent_live, "w_embed": w_embed, "gain_attn": gain_attn, "w_qkv": w_qkv, "w_out": w_out, "gain_mlp": gain_mlp, "w_up": w_up, "w_down": w_down}


EPS = 1e-06
SCORE_SCALE = 3.0

def conv_same(grid, kernel):
    height, breadth, channels = grid.shape
    padded = jnp.pad(grid.astype(jnp.float32), ((1, 1), (1, 1), (0, 0)))
    kernel_f = kernel.astype(jnp.float32)
    summed = jnp.zeros((height * breadth, kernel.shape[3]), jnp.float32)
    for offset_r in range(3):
        for offset_c in range(3):
            window = padded[offset_r:offset_r + height, offset_c:offset_c + breadth].reshape(-1, channels)
            summed = summed + jnp.dot(window, kernel_f[offset_r, offset_c], precision=lax.Precision.HIGHEST)
    return summed.reshape(height, breadth, -1)

def pool_crops(crop_block):
    leading = crop_block.shape[:-3]
    side_len = CROP // POOL
    channels = crop_block.shape[-1]
    shaped = crop_block.reshape(leading + (side_len, POOL, side_len, POOL, channels)).astype(jnp.float32)
    pool_means = lax.optimization_barrier(jnp.mean(shaped, axis=(-4, -2)))
    return pool_means.reshape(leading + (side_len * side_len * channels,)).astype(jnp.bfloat16)

def rms_scaled(values, gain_vec):
    return values * lax.rsqrt(lax.optimization_barrier(jnp.mean(values * values, axis=-1, keepdims=True)) + EPS) * gain_vec

def unit_heads(values):
    shaped = values.reshape(values.shape[0], HEADS, -1)
    return (shaped * lax.rsqrt(lax.optimization_barrier(jnp.mean(shaped * shaped, axis=-1, keepdims=True)) + EPS)).astype(jnp.bfloat16)

def reference(raster, conv_first, conv_second, crop_anchor, agent_live, w_embed, gain_attn, w_qkv, w_out, gain_mlp, w_up, w_down):
    first_layer = jax.nn.relu(conv_same(raster, conv_first)).astype(jnp.bfloat16)
    features = (raster.astype(jnp.float32) + conv_same(first_layer, conv_second)).astype(jnp.bfloat16)
    channels = features.shape[2]
    slot_ids = jnp.arange(AGENT_SLOTS, dtype=jnp.int32)
    shard_ids = slot_ids // SLOTS
    within = slot_ids % SLOTS
    band_ids = shard_ids // GRID_COLS
    dest_ids = shard_ids % GRID_COLS
    owner_ids = within // CAP
    rank_ids = within % CAP
    source = ((band_ids * GRID_COLS + owner_ids) * SLOTS + dest_ids * CAP + rank_ids).astype(jnp.int32)
    top_cells = crop_anchor[0][source].astype(jnp.int32)
    left_cells = crop_anchor[1][source].astype(jnp.int32)

    def cut_one(top_cell, left_cell):
        return lax.dynamic_slice(features, (top_cell, left_cell, jnp.int32(0)), (CROP, CROP, channels))
    pooled = pool_crops(jax.vmap(cut_one)(top_cells, left_cells))
    embedded = jnp.dot(pooled, w_embed, preferred_element_type=jnp.float32)
    normed_attn = rms_scaled(embedded, gain_attn).astype(jnp.bfloat16)
    model_width = embedded.shape[1]
    projected = jnp.dot(normed_attn, w_qkv, preferred_element_type=jnp.float32)
    unit_q = unit_heads(projected[:, :model_width])
    unit_k = unit_heads(projected[:, model_width:2 * model_width])
    values = projected[:, 2 * model_width:].astype(jnp.bfloat16).reshape(AGENT_SLOTS, HEADS, -1)
    live_float = agent_live.astype(jnp.float32)
    factor = SCORE_SCALE / HEAD_DIM ** 0.5

    def one_head(operands):
        q_head, k_head, v_head = operands
        scores = jnp.dot(q_head.astype(jnp.float32), k_head.astype(jnp.float32).T, precision=lax.Precision.HIGHEST) * factor
        weights = (jnp.exp(scores) * live_float[None, :]).astype(jnp.bfloat16)
        numerator = jnp.dot(weights.astype(jnp.float32), v_head.astype(jnp.float32), precision=lax.Precision.HIGHEST)
        denominator = lax.optimization_barrier(jnp.sum(weights.astype(jnp.float32), axis=1))
        return numerator / denominator[:, None]
    per_head = lax.map(one_head, (unit_q.transpose(1, 0, 2), unit_k.transpose(1, 0, 2), values.transpose(1, 0, 2)))
    attended = per_head.transpose(1, 0, 2).reshape(AGENT_SLOTS, model_width).astype(jnp.bfloat16)
    after_attn = embedded + jnp.dot(attended, w_out, preferred_element_type=jnp.float32)
    normed_mlp = rms_scaled(after_attn, gain_mlp).astype(jnp.bfloat16)
    activated = jax.nn.gelu(jnp.dot(normed_mlp, w_up, preferred_element_type=jnp.float32)).astype(jnp.bfloat16)
    agent_out = ((after_attn + jnp.dot(activated, w_down, preferred_element_type=jnp.float32)) * live_float[:, None]).astype(jnp.bfloat16)
    return (features, agent_out)
```

```python
import jax
import jax.numpy as jnp
from jax import lax
from jax.experimental import pallas as pl
from jax.experimental.pallas import tpu as pltpu
from jax.sharding import PartitionSpec as P

HEADS = 8
HEAD_DIM = 64
CROP = 16
EPS = 1e-06
SCORE_SCALE = 3.0

ROWS, COLS, CH = 128, 64, 128
NEAR, FAR = 2, 17
SLOTS_X = 76
PAIRS_1 = 75
PAIRS_2 = 72
NB1, NB2 = 5, 4
WIDE_1, WIDE_2 = 96, 80
F32, BF16 = jnp.float32, jnp.bfloat16


def dot(a, b):
    return lax.dot_general(a, b, (((1,), (0,)), ((), ())), preferred_element_type=F32)


def dot_t(a, b):
    return lax.dot_general(a, b, (((1,), (1,)), ((), ())), preferred_element_type=F32)


def iota(shape, dim):
    return lax.broadcasted_iota(jnp.int32, shape, dim)


def band(kernel_ref, band_ref):
    zero = jnp.zeros((CH, CH), BF16)
    for a in range(4):
        for b in range(3):
            at = pl.ds((a * 3 + b) * CH, CH)
            band_ref[at, 0:CH] = kernel_ref[a * 3 + b] if a < 3 else zero
            band_ref[at, CH : 2 * CH] = kernel_ref[(a - 1) * 3 + b] if a > 0 else zero


def scene_kernel(
    anchor_ref,
    raster_hbm,
    above_hbm,
    below_hbm,
    left_ref,
    right_ref,
    conv1_ref,
    conv2_ref,
    flags_ref,
    gain_ref,
    w_embed_hbm,
    w_qkv_hbm,
    features_hbm,
    payload_ref,
    center,
    shifted_1,
    shifted_2,
    row_wide,
    row_first,
    wide_features,
    out_features,
    band_1,
    band_2,
    block_sum,
    pooled,
    w_embed,
    w_qkv,
    in_sem,
    w_sem,
    out_sem,
):
    row_id = lax.axis_index("row")
    col_id = lax.axis_index("col")
    copies = [
        pltpu.make_async_copy(above_hbm, center.at[pl.ds(0, NEAR)], in_sem.at[0]),
        pltpu.make_async_copy(raster_hbm, center.at[pl.ds(NEAR, ROWS)], in_sem.at[1]),
        pltpu.make_async_copy(below_hbm, center.at[pl.ds(NEAR + ROWS, FAR)], in_sem.at[2]),
    ]
    for copy in copies:
        copy.start()
    weight_copies = [
        pltpu.make_async_copy(w_embed_hbm, w_embed, w_sem.at[0]),
        pltpu.make_async_copy(w_qkv_hbm, w_qkv, w_sem.at[1]),
    ]
    for copy in weight_copies:
        copy.start()
    band(conv1_ref, band_1)
    band(conv2_ref, band_2)
    known = NEAR + ROWS + FAR
    center[pl.ds(known, 2 * SLOTS_X - known)] = jnp.zeros((2 * SLOTS_X - known, COLS, CH), BF16)
    row_wide[...] = jnp.zeros(row_wide.shape, F32)
    for copy in copies:
        copy.wait()

    def spread(slot, _):
        for par in range(2):
            u = slot * 2 + par
            safe = jnp.minimum(u, known - 1)
            row_wide[par, 14:16] = left_ref[safe].astype(F32)
            row_wide[par, 16:80] = center[u].astype(F32)
            row_wide[par, 80 : 80 + FAR] = right_ref[safe].astype(F32)
        for par in range(2):
            for b in range(3):
                lane = (par * 3 + b) * CH
                shifted_1[slot, :, lane : lane + CH] = row_wide[
                    par, 7 + b : 7 + b + WIDE_1
                ].astype(BF16)
        return _

    lax.fori_loop(0, SLOTS_X, spread, 0)

    column = col_id * COLS - 8 + iota((WIDE_1, CH), 0)
    column_in = (column >= 0) & (column < COLS * 16)

    def first(block, _):
        p0 = block * NB1
        low = shifted_1[pl.ds(p0, NB1)].reshape(NB1 * WIDE_1, 6 * CH)
        high = shifted_1[pl.ds(p0 + 1, NB1)].reshape(NB1 * WIDE_1, 6 * CH)
        total = dot(low, band_1[0 : 6 * CH]) + dot(high, band_1[6 * CH :])
        for i in range(NB1):
            for par in range(2):
                rho = row_id * ROWS - 1 + (p0 + i) * 2 + par
                row_in = (rho >= 0) & (rho < ROWS * 8)
                value = total[i * WIDE_1 : (i + 1) * WIDE_1, par * CH : (par + 1) * CH]
                keep = column_in & row_in
                row_first[2 * i + par] = jnp.where(keep, jnp.maximum(value, 0.0), 0.0)
        for i in range(NB1):
            for par in range(2):
                for b in range(3):
                    lane = (par * 3 + b) * CH
                    shifted_2[p0 + i, :, lane : lane + CH] = row_first[
                        2 * i + par, 7 + b : 7 + b + WIDE_2
                    ].astype(BF16)
        return _

    lax.fori_loop(0, PAIRS_1 // NB1, first, 0)

    def second(block, _):
        p0 = block * NB2
        low = shifted_2[pl.ds(p0, NB2)].reshape(NB2 * WIDE_2, 6 * CH)
        high = shifted_2[pl.ds(p0 + 1, NB2)].reshape(NB2 * WIDE_2, 6 * CH)
        total = dot(low, band_2[0 : 6 * CH]) + dot(high, band_2[6 * CH :])
        for i in range(NB2):
            for par in range(2):
                lane = (par * 3 + 1) * CH
                base = shifted_1[p0 + i + 1, :, lane : lane + CH].astype(F32)[8 : 8 + WIDE_2]
                value = total[i * WIDE_2 : (i + 1) * WIDE_2, par * CH : (par + 1) * CH] + base
                value = value.astype(BF16)
                at = pl.multiple_of(((p0 + i) * 2 + par) * WIDE_2, WIDE_2)
                wide_features[pl.ds(at, WIDE_2)] = value.astype(F32)
                out_features[(p0 + i) * 2 + par] = value[:COLS]
        return _

    lax.fori_loop(0, PAIRS_2 // NB2, second, 0)
    out_copy = pltpu.make_async_copy(out_features.at[pl.ds(0, ROWS)], features_hbm, out_sem)
    out_copy.start()

    def crop(agent, _):
        top = anchor_ref[0, agent] - row_id * ROWS
        left = anchor_ref[1, agent] - col_id * COLS
        for rb in range(4):
            start = (top + rb * 4) * WIDE_2 + left
            four = [wide_features[pl.ds(start + i * WIDE_2, CROP)] for i in range(4)]
            block_sum[rb] = (four[0] + four[1]) + (four[2] + four[3])
        for rb in range(4):
            cells = [block_sum[rb, pl.ds(k, 4, stride=4)] for k in range(4)]
            mean = ((cells[0] + cells[1]) + (cells[2] + cells[3])) * (1.0 / 16)
            pooled[pl.ds(rb * 4 * 32 + agent, 4, stride=32)] = mean
        return _

    lax.fori_loop(0, 32, crop, 0)
    for copy in weight_copies:
        copy.wait()
    agents = jnp.concatenate(
        [pooled[b * 32 : (b + 1) * 32].astype(BF16) for b in range(16)], axis=1
    )
    embedded = dot(agents, w_embed[...])
    power = jnp.mean(embedded * embedded, axis=1, keepdims=True)
    normed = (embedded * lax.rsqrt(power + EPS) * gain_ref[...]).astype(BF16)
    projected = dot(normed, w_qkv[...])
    lane_id = iota((32, CH), 1)
    lower = lane_id < HEAD_DIM

    def unit(x):
        squared = x * x
        first_half = jnp.sum(jnp.where(lower, squared, 0.0), axis=1, keepdims=True)
        second_half = jnp.sum(jnp.where(lower, 0.0, squared), axis=1, keepdims=True)
        scale = lax.rsqrt(jnp.where(lower, first_half, second_half) * (1.0 / HEAD_DIM) + EPS)
        return x * scale

    def turned(x):
        return pltpu.roll(x, HEAD_DIM, 1)

    shift = lax.rem(col_id // 4, 4)
    for pair in range(4):
        q_two = unit(projected[:, pair * CH : (pair + 1) * CH])
        k_two = unit(projected[:, 512 + pair * CH : 512 + (pair + 1) * CH])
        v_two = projected[:, 1024 + pair * CH : 1024 + (pair + 1) * CH]
        rolled = (turned(q_two), turned(k_two), turned(v_two))
        for half in range(2):
            h = pair * 2 + half
            q_h = rolled[0] if half else q_two
            k_h = rolled[1] if half else k_two
            v_h = v_two if half else rolled[2]
            kv = jnp.where(lower, k_h, v_h)
            for kp in range(4):
                chunk = h * 4 + kp
                source = embedded[:, (chunk // 8) * CH : (chunk // 8 + 1) * CH]
                offset = (chunk % 8) * 16
                piece = pltpu.roll(source, (HEAD_DIM - offset) % CH, 1)
                high = piece.astype(BF16).astype(F32)
                low = pltpu.roll(piece - high, 16, 1)
                extra = jnp.where(
                    lane_id < 80, high, jnp.where(lane_id < 96, low, flags_ref[...])
                )
                row = jnp.where(lower, q_h, extra)
                for gg in range(4):
                    g = lax.rem(gg + shift, 4)
                    both = jnp.concatenate(
                        [kv[kp * 8 : kp * 8 + 8], row[gg * 8 : gg * 8 + 8]], axis=0
                    )
                    payload_ref[chunk * 4 + g] = both.astype(BF16)
    out_copy.wait()


def attend_kernel(received_ref, out_ref, queries, partial):
    device = lax.axis_index("row") * 16 + lax.axis_index("col")
    quarter = lax.rem(device // 4, 4)
    g = lax.rem(device, 4)
    everything = received_ref[...].astype(F32)
    kv = everything[:, 0:8].reshape(1024, CH)
    q_rows = everything[:, 8:16].reshape(1024, CH)
    queries[...] = q_rows
    flags = queries[pl.ds(0, 128, stride=8)].astype(BF16)
    key = iota((1024, CH), 0)
    lane = iota((1024, CH), 1)
    source = (key // 128) * 16 + quarter * 4 + lax.rem(key // 2, 4)
    chosen = dot((lane == source).astype(F32).astype(BF16), flags)
    wanted = 96 + lax.rem(key // 8, 16) * 2 + lax.rem(key, 2)
    alone = jnp.where(lane == wanted, chosen, 0.0).astype(BF16)
    mask = dot(alone, jnp.ones((CH, CH), BF16))
    lower = lane < HEAD_DIM
    keys = jnp.where(lower, kv, 0.0).astype(BF16)
    values = (jnp.where(lower, 1.0, kv) * mask).astype(BF16)
    factor = SCORE_SCALE / HEAD_DIM**0.5
    step = 256
    lane_s = iota((step, CH), 1)
    for i in range(1024 // step):
        q = queries[i * step : (i + 1) * step]
        weights = jnp.exp(dot_t(q.astype(BF16), keys) * factor).astype(BF16)
        summed = pltpu.roll(dot(weights, values), HEAD_DIM, 1)
        high = summed.astype(BF16).astype(F32)
        partial[i * step : (i + 1) * step] = jnp.where(
            lane_s < HEAD_DIM,
            summed,
            jnp.where(lane_s < 96, q, jnp.where(lane_s < 112, high, summed - high)),
        )
    for r in range(8):
        for oh in range(4):
            dh = lax.rem(g - oh + 4, 4)
            for dl in range(4):
                base = (r * 4 + oh) * 32 + dl * 2
                rows = [partial[pl.ds(base + k, 4, stride=8)] for k in range(2)]
                out_ref[r * 16 + dh * 4 + dl] = jnp.concatenate(rows, axis=0).astype(BF16)


def agent_kernel(returned_ref, live_ref, gain_ref, w_out, w_up, w_down, out_ref):
    lane = iota((32, CH), 1)
    lower = lane < HEAD_DIM
    everything = returned_ref[...].astype(F32)
    attended = []
    embedded = []
    chunk_sum = None
    for h in range(HEADS):
        total = None
        for kp in range(4):
            chunk = h * 4 + kp
            block = everything[chunk * 4 : chunk * 4 + 4].reshape(32, CH)
            total = block if total is None else total + block
            whole = block + pltpu.roll(block, CH - 16, 1)
            placed = pltpu.roll(whole, (chunk % 8 * 16 - HEAD_DIM) % CH, 1)
            here = (lane // 16) == chunk % 8
            chunk_sum = jnp.where(here, placed, 0.0 if chunk % 8 == 0 else chunk_sum)
            if chunk % 8 == 7:
                embedded.append(chunk_sum)
        below = jnp.sum(jnp.where((lane == 96) | (lane == 112), total, 0.0), axis=1, keepdims=True)
        ratio = total / below
        if h % 2 == 0:
            even = ratio
        else:
            attended.append(jnp.where(lower, even, pltpu.roll(ratio, HEAD_DIM, 1)).astype(BF16))
    attended = jnp.concatenate(attended, axis=1)
    embedded = jnp.concatenate(embedded, axis=1)
    after = embedded + dot(attended, w_out[...])
    power = jnp.mean(after * after, axis=1, keepdims=True)
    normed = (after * lax.rsqrt(power + EPS) * gain_ref[...]).astype(BF16)
    activated = jax.nn.gelu(dot(normed, w_up[...])).astype(BF16)
    result = (after + dot(activated, w_down[...])).astype(BF16)
    dh = lax.axis_index("col") // 4
    slot = iota((32, 32), 0)
    at = iota((32, 32), 1)
    g = lax.rem(slot // 8 + dh, 4)
    place = g * 8 + lax.rem(slot, 2) * 4 + lax.rem(slot // 2, 4)
    order = (at == place).astype(F32).astype(BF16)
    out_ref[...] = (dot(order, result) * live_ref[...]).astype(BF16)


VMEM = pl.BlockSpec(memory_space=pltpu.VMEM)
SMEM = pl.BlockSpec(memory_space=pltpu.SMEM)
ANY = pl.BlockSpec(memory_space=pl.ANY)


def scene(anchor, raster, above, below, left, right, conv1, conv2, flags, gain, w_embed, w_qkv):
    return pl.pallas_call(
        scene_kernel,
        out_shape=(
            jax.ShapeDtypeStruct((ROWS, COLS, CH), BF16),
            jax.ShapeDtypeStruct((128, 16, CH), BF16),
        ),
        in_specs=[SMEM, ANY, ANY, ANY, VMEM, VMEM, VMEM, VMEM, VMEM, VMEM, ANY, ANY],
        out_specs=(ANY, VMEM),
        scratch_shapes=[
            pltpu.VMEM((2 * SLOTS_X, COLS, CH), BF16),
            pltpu.VMEM((SLOTS_X, WIDE_1, 6 * CH), BF16),
            pltpu.VMEM((SLOTS_X, WIDE_2, 6 * CH), BF16),
            pltpu.VMEM((2, 112, CH), F32),
            pltpu.VMEM((2 * NB1, WIDE_1, CH), F32),
            pltpu.VMEM((2 * PAIRS_2 * WIDE_2, CH), F32),
            pltpu.VMEM((2 * PAIRS_2, COLS, CH), BF16),
            pltpu.VMEM((12 * CH, 2 * CH), BF16),
            pltpu.VMEM((12 * CH, 2 * CH), BF16),
            pltpu.VMEM((4, CROP, CH), F32),
            pltpu.VMEM((16 * 32, CH), F32),
            pltpu.VMEM(w_embed.shape, BF16),
            pltpu.VMEM(w_qkv.shape, BF16),
            pltpu.SemaphoreType.DMA((3,)),
            pltpu.SemaphoreType.DMA((2,)),
            pltpu.SemaphoreType.DMA,
        ],
        compiler_params=pltpu.CompilerParams(vmem_limit_bytes=56 * 2**20),
        cost_estimate=pl.CostEstimate(flops=10**10, bytes_accessed=10**7, transcendentals=0),
        name="scene",
    )(anchor, raster, above, below, left, right, conv1, conv2, flags, gain, w_embed, w_qkv)


def attend(received):
    return pl.pallas_call(
        attend_kernel,
        out_shape=jax.ShapeDtypeStruct((128, 8, CH), BF16),
        in_specs=[VMEM],
        out_specs=VMEM,
        scratch_shapes=[pltpu.VMEM((1024, CH), F32), pltpu.VMEM((1024, CH), F32)],
        compiler_params=pltpu.CompilerParams(vmem_limit_bytes=40 * 2**20),
        name="attend",
    )(received)


def finish(returned, live, gain, w_out, w_up, w_down):
    return pl.pallas_call(
        agent_kernel,
        out_shape=jax.ShapeDtypeStruct((32, 512), BF16),
        in_specs=[VMEM] * 6,
        out_specs=VMEM,
        compiler_params=pltpu.CompilerParams(vmem_limit_bytes=40 * 2**20),
        name="agents",
    )(returned, live, gain, w_out, w_up, w_down)


def per_device(
    raster,
    conv_first,
    conv_second,
    crop_anchor,
    agent_live,
    w_embed,
    gain_attn,
    w_qkv,
    w_out,
    gain_mlp,
    w_up,
    w_down,
):
    def forward(n):
        return [(i, i + 1) for i in range(n - 1)]

    def backward(n):
        return [(i + 1, i) for i in range(n - 1)]

    above = lax.ppermute(raster[-NEAR:], "row", forward(8))
    below = lax.ppermute(raster[:FAR], "row", backward(8))
    last = jnp.concatenate([above[:, -NEAR:], raster[:, -NEAR:], below[:, -NEAR:]], axis=0)
    initial = jnp.concatenate([above[:, :FAR], raster[:, :FAR], below[:, :FAR]], axis=0)
    left = lax.ppermute(last, "col", forward(16))
    right = lax.ppermute(initial, "col", backward(16))
    flags = jnp.pad(agent_live.astype(F32)[None], ((0, 0), (96, 0)))
    features, payload = scene(
        crop_anchor,
        raster,
        above,
        below,
        left,
        right,
        conv_first.reshape(9, CH, CH),
        conv_second.reshape(9, CH, CH),
        flags,
        gain_attn[None],
        w_embed,
        w_qkv,
    )
    received = lax.all_to_all(payload, ("row", "col"), 0, 0, tiled=True)
    returned = lax.all_to_all(attend(received), ("row", "col"), 0, 0, tiled=True)
    live = agent_live.astype(F32)[:, None]
    agent_out = finish(returned, live, gain_mlp[None], w_out, w_up, w_down)
    return (features, agent_out)


def solution(mesh):
    in_specs = (
        P("row", "col", None),
        P(),
        P(),
        P(None, ("row", "col")),
        P(("row", "col")),
        P(),
        P(),
        P(),
        P(),
        P(),
        P(),
        P(),
    )
    out_specs = (P("row", "col", None), P(("row", "col"), None))
    return jax.shard_map(
        per_device, mesh=mesh, in_specs=in_specs, out_specs=out_specs, check_vma=False
    )
```

```python
import jax
import jax.numpy as jnp
from jax import lax
from jax.experimental import pallas as pl
from jax.experimental.pallas import tpu as pltpu
from jax.experimental.layout import Layout, with_layout_constraint
from jax.sharding import PartitionSpec as P

HEADS = 8
HEAD_DIM = 64
CROP = 16
EPS = 1e-06
SCORE_SCALE = 3.0

ROWS, COLS, CH = 128, 64, 128
NEAR, FAR = 2, 17
KNOWN = NEAR + ROWS + FAR
PAIRS_1 = 76
PAIRS_2 = 72
SLOTS = 77
NB1, NB2, NBS = 19, 18, 38
WIDE = 80
STRIP = 32
TAPS = ((0, 0), (0, 2), (1, 0), (1, 2), (0, 1), (1, 1))
F32, BF16 = jnp.float32, jnp.bfloat16


def dot(a, b):
    return lax.dot_general(a, b, (((1,), (0,)), ((), ())), preferred_element_type=F32)


def dot_t(a, b):
    return lax.dot_general(a, b, (((1,), (1,)), ((), ())), preferred_element_type=F32)


def iota(shape, dim):
    return lax.broadcasted_iota(jnp.int32, shape, dim)


def band(kernel_ref, band_ref):
    zero = jnp.zeros((CH, CH), BF16)
    for slot in range(2):
        for i, (par, b) in enumerate(TAPS):
            a = slot * 2 + par
            at = pl.ds((slot * 6 + i) * CH, CH)
            band_ref[at, 0:CH] = kernel_ref[a * 3 + b] if a < 3 else zero
            band_ref[at, CH : 2 * CH] = kernel_ref[(a - 1) * 3 + b] if a > 0 else zero


def load_center(raster_hbm, above_hbm, below_hbm, center, sems):
    return [
        pltpu.make_async_copy(above_hbm, center.at[pl.ds(0, NEAR)], sems.at[0]),
        pltpu.make_async_copy(raster_hbm, center.at[pl.ds(NEAR, ROWS)], sems.at[1]),
        pltpu.make_async_copy(below_hbm, center.at[pl.ds(NEAR + ROWS, FAR)], sems.at[2]),
    ]


def row_inside(rho):
    return (rho >= 0) & (rho < ROWS * 8)


def first_kernel(
    raster_hbm,
    above_hbm,
    below_hbm,
    conv1_ref,
    inner_hbm,
    center,
    shifted_a,
    shifted_b,
    row_wide,
    inner,
    band_1,
    in_sem,
    out_sem,
):
    row_id = lax.axis_index("row")
    copies = load_center(raster_hbm, above_hbm, below_hbm, center, in_sem)
    for copy in copies:
        copy.start()
    band(conv1_ref, band_1)
    center[pl.ds(KNOWN, 2 * SLOTS - KNOWN)] = jnp.zeros((2 * SLOTS - KNOWN, COLS, CH), BF16)
    row_wide[:, 0:8] = jnp.zeros((2 * NB1 + 2, 8, CH), F32)
    row_wide[:, 72:80] = jnp.zeros((2 * NB1 + 2, 8, CH), F32)
    for copy in copies:
        copy.wait()

    def spread(block, shifted):
        for i in range(NB1 + 1):
            for par in range(2):
                wide = row_wide.at[2 * i + par]
                wide[8:72] = center[(block * NB1 + i) * 2 + par].astype(F32)
                shifted[i, :, (par * 2) * CH : (par * 2 + 1) * CH] = wide[7:71].astype(BF16)
                shifted[i, :, (par * 2 + 1) * CH : (par * 2 + 2) * CH] = wide[9:73].astype(BF16)

    def multiply(block, shifted):
        def side(s):
            plain = center[pl.ds((block * NB1 + s) * 2, 2 * NB1)].reshape(NB1, 2, COLS, CH)
            parts = [shifted[s : s + NB1], plain[:, 0], plain[:, 1]]
            return jnp.concatenate(parts, axis=2).reshape(NB1 * COLS, 6 * CH)

        total = dot(side(0), band_1[0 : 6 * CH]) + dot(side(1), band_1[6 * CH :])
        total = jnp.maximum(total, 0.0)
        for i in range(NB1):
            for par in range(2):
                v = (block * NB1 + i) * 2 + par
                value = total[i * COLS : (i + 1) * COLS, par * CH : (par + 1) * CH]
                value = jnp.where(row_inside(row_id * ROWS - 1 + v), value, 0.0)
                inner[v] = value.astype(BF16)

    blocks = PAIRS_1 // NB1
    buffers = (shifted_a, shifted_b)
    spread(0, buffers[0])
    copies = []
    for block in range(blocks):
        multiply(block, buffers[block % 2])
        if block + 1 < blocks:
            spread(block + 1, buffers[(block + 1) % 2])
        part = pl.ds(block * NB1 * 2, NB1 * 2)
        copies.append(pltpu.make_async_copy(inner.at[part], inner_hbm.at[part], out_sem.at[block]))
        copies[-1].start()
    for copy in copies:
        copy.wait()


def scene_kernel(
    anchor_ref,
    raster_hbm,
    above_hbm,
    below_hbm,
    left_ref,
    right_ref,
    inner_hbm,
    conv1_ref,
    conv2_ref,
    flags_ref,
    gain_ref,
    w_embed_hbm,
    w_qkv_hbm,
    features_hbm,
    payload_ref,
    center,
    inner,
    edge_wide,
    edge_shifted,
    edge_first,
    row_first,
    shifted_a,
    shifted_b,
    wide_features,
    out_features,
    band_1,
    band_2,
    block_sum,
    pooled,
    w_embed,
    w_qkv,
    in_sem,
    w_sem,
    out_sem,
):
    row_id = lax.axis_index("row")
    col_id = lax.axis_index("col")
    copies = load_center(raster_hbm, above_hbm, below_hbm, center, in_sem)
    for copy in copies:
        copy.start()
    inner_copy = pltpu.make_async_copy(inner_hbm, inner, in_sem.at[3])
    inner_copy.start()
    weight_copies = [
        pltpu.make_async_copy(w_embed_hbm, w_embed, w_sem.at[0]),
        pltpu.make_async_copy(w_qkv_hbm, w_qkv, w_sem.at[1]),
    ]
    for copy in weight_copies:
        copy.start()
    band(conv1_ref, band_1)
    band(conv2_ref, band_2)
    center[pl.ds(KNOWN, 2 * SLOTS - KNOWN)] = jnp.zeros((2 * SLOTS - KNOWN, COLS, CH), BF16)
    edge_wide[pl.ds(KNOWN * 64, (2 * SLOTS - KNOWN) * 64)] = jnp.zeros(
        ((2 * SLOTS - KNOWN) * 64, CH), F32
    )
    for c in range(NEAR):
        edge_wide[pl.ds(6 + c, KNOWN, stride=64)] = left_ref[c].astype(F32)
    for c in range(FAR):
        edge_wide[pl.ds(32 + c, KNOWN, stride=64)] = right_ref[c].astype(F32)
    for copy in copies:
        copy.wait()

    def edges(slot, _):
        for par in range(2):
            u = slot * 2 + par
            wide = edge_wide.at[pl.ds(pl.multiple_of(u * 64, 64), 64)]
            wide[8:16] = center[u, 0:16].astype(F32)[0:8]
            wide[24:32] = center[u, 48:64].astype(F32)[8:16]
            wide[49:64] = jnp.zeros((15, CH), F32)
        for i, (par, b) in enumerate(TAPS):
            wide = edge_wide.at[pl.ds(pl.multiple_of((slot * 2 + par) * 64, 64), 64)]
            both = jnp.concatenate([wide[6 + b : 14 + b], wide[30 + b : 54 + b]], axis=0)
            edge_shifted[slot, :, i * CH : (i + 1) * CH] = both.astype(BF16)
        return _

    lax.fori_loop(0, SLOTS, edges, 0, unroll=7)
    strip = iota((STRIP, CH), 0)
    column = col_id * COLS + jnp.where(strip < 8, strip - 1, strip + 55)
    column_in = (column >= 0) & (column < COLS * 16)

    def edge_multiply(block, _):
        p0 = block * NBS

        def side(s):
            return edge_shifted[pl.ds(p0 + s, NBS)].reshape(NBS * STRIP, 6 * CH)

        total = dot(side(0), band_1[0 : 6 * CH]) + dot(side(1), band_1[6 * CH :])
        total = jnp.maximum(total, 0.0)
        for i in range(NBS):
            for par in range(2):
                v = (p0 + i) * 2 + par
                value = total[i * STRIP : (i + 1) * STRIP, par * CH : (par + 1) * CH]
                keep = column_in & row_inside(row_id * ROWS - 1 + v)
                edge_first[v] = jnp.where(keep, value, 0.0)
        return _

    lax.fori_loop(0, PAIRS_1 // NBS, edge_multiply, 0)
    inner_copy.wait()

    def assemble(block, shifted):
        for i in range(NB2 + 1):
            for par in range(2):
                v = (block * NB2 + i) * 2 + par
                first = row_first.at[2 * i + par]
                first[8:72] = inner[v].astype(F32)
                first[7:9] = edge_first[v, 0:2]
                first[71:95] = edge_first[v, 8:32]
            for k, (par, b) in enumerate(TAPS):
                window = row_first[2 * i + par, 7 + b : 7 + b + WIDE]
                shifted[i, :, k * CH : (k + 1) * CH] = window.astype(BF16)

    def multiply(block, shifted):
        def side(s):
            return shifted[s : s + NB2].reshape(NB2 * WIDE, 6 * CH)

        total = dot(side(0), band_2[0 : 6 * CH]) + dot(side(1), band_2[6 * CH :])
        for i in range(NB2):
            for par in range(2):
                row = (block * NB2 + i) * 2 + par
                u = row + NEAR
                right = edge_wide[u * 64 + 32 : u * 64 + 48]
                base = jnp.concatenate([center[u].astype(F32), right], axis=0)
                value = total[i * WIDE : (i + 1) * WIDE, par * CH : (par + 1) * CH] + base
                value = value.astype(BF16)
                wide_features[row * WIDE : (row + 1) * WIDE] = value.astype(F32)
                out_features[row] = value[:COLS]

    blocks = PAIRS_2 // NB2
    buffers = (shifted_a, shifted_b)
    assemble(0, buffers[0])
    for block in range(blocks):
        multiply(block, buffers[block % 2])
        if block + 1 < blocks:
            assemble(block + 1, buffers[(block + 1) % 2])
    out_copy = pltpu.make_async_copy(out_features.at[pl.ds(0, ROWS)], features_hbm, out_sem)
    out_copy.start()

    def crop(agent, _):
        top = anchor_ref[0, agent] - row_id * ROWS
        left = anchor_ref[1, agent] - col_id * COLS
        for rb in range(4):
            start = (top + rb * 4) * WIDE + left
            four = [wide_features[pl.ds(start + i * WIDE, CROP)] for i in range(4)]
            block_sum[rb] = (four[0] + four[1]) + (four[2] + four[3])
        for rb in range(4):
            cells = [block_sum[rb, pl.ds(k, 4, stride=4)] for k in range(4)]
            mean = ((cells[0] + cells[1]) + (cells[2] + cells[3])) * (1.0 / 16)
            pooled[pl.ds(rb * 4 * 32 + agent, 4, stride=32)] = mean
        return _

    lax.fori_loop(0, 32, crop, 0)
    for copy in weight_copies:
        copy.wait()
    agents = jnp.concatenate(
        [pooled[b * 32 : (b + 1) * 32].astype(BF16) for b in range(16)], axis=1
    )
    embedded = dot(agents, w_embed[...])
    power = jnp.mean(embedded * embedded, axis=1, keepdims=True)
    normed = (embedded * lax.rsqrt(power + EPS) * gain_ref[...]).astype(BF16)
    projected = dot(normed, w_qkv[...])
    lane_id = iota((32, CH), 1)
    lower = lane_id < HEAD_DIM

    def unit(x):
        squared = x * x
        first_half = jnp.sum(jnp.where(lower, squared, 0.0), axis=1, keepdims=True)
        second_half = jnp.sum(jnp.where(lower, 0.0, squared), axis=1, keepdims=True)
        scale = lax.rsqrt(jnp.where(lower, first_half, second_half) * (1.0 / HEAD_DIM) + EPS)
        return x * scale

    def turned(x):
        return pltpu.roll(x, HEAD_DIM, 1)

    shift = lax.rem(col_id // 4, 4)
    for pair in range(4):
        q_two = unit(projected[:, pair * CH : (pair + 1) * CH])
        k_two = unit(projected[:, 512 + pair * CH : 512 + (pair + 1) * CH])
        v_two = projected[:, 1024 + pair * CH : 1024 + (pair + 1) * CH]
        rolled = (turned(q_two), turned(k_two), turned(v_two))
        for half in range(2):
            h = pair * 2 + half
            q_h = rolled[0] if half else q_two
            k_h = rolled[1] if half else k_two
            v_h = v_two if half else rolled[2]
            kv = jnp.where(lower, k_h, v_h)
            for kp in range(4):
                chunk = h * 4 + kp
                source = embedded[:, (chunk // 8) * CH : (chunk // 8 + 1) * CH]
                offset = (chunk % 8) * 16
                piece = pltpu.roll(source, (HEAD_DIM - offset) % CH, 1)
                high = piece.astype(BF16).astype(F32)
                low = pltpu.roll(piece - high, 16, 1)
                extra = jnp.where(
                    lane_id < 80, high, jnp.where(lane_id < 96, low, flags_ref[...])
                )
                row = jnp.where(lower, q_h, extra)
                for gg in range(4):
                    g = lax.rem(gg + shift, 4)
                    both = jnp.concatenate(
                        [kv[kp * 8 : kp * 8 + 8], row[gg * 8 : gg * 8 + 8]], axis=0
                    )
                    payload_ref[chunk * 4 + g] = both.astype(BF16)
    out_copy.wait()


def attend_kernel(received_ref, out_ref, queries, partial):
    device = lax.axis_index("row") * 16 + lax.axis_index("col")
    quarter = lax.rem(device // 4, 4)
    g = lax.rem(device, 4)
    everything = received_ref[...].astype(F32)
    kv = everything[:, 0:8].reshape(1024, CH)
    q_rows = everything[:, 8:16].reshape(1024, CH)
    queries[...] = q_rows
    flags = queries[pl.ds(0, 128, stride=8)].astype(BF16)
    key = iota((1024, CH), 0)
    lane = iota((1024, CH), 1)
    source = (key // 128) * 16 + quarter * 4 + lax.rem(key // 2, 4)
    chosen = dot((lane == source).astype(F32).astype(BF16), flags)
    wanted = 96 + lax.rem(key // 8, 16) * 2 + lax.rem(key, 2)
    alone = jnp.where(lane == wanted, chosen, 0.0).astype(BF16)
    mask = dot(alone, jnp.ones((CH, CH), BF16))
    lower = lane < HEAD_DIM
    keys = jnp.where(lower, kv, 0.0).astype(BF16)
    values = (jnp.where(lower, 1.0, kv) * mask).astype(BF16)
    factor = SCORE_SCALE / HEAD_DIM**0.5
    step = 256
    lane_s = iota((step, CH), 1)
    for i in range(1024 // step):
        q = queries[i * step : (i + 1) * step]
        weights = jnp.exp(dot_t(q.astype(BF16), keys) * factor).astype(BF16)
        summed = pltpu.roll(dot(weights, values), HEAD_DIM, 1)
        high = summed.astype(BF16).astype(F32)
        partial[i * step : (i + 1) * step] = jnp.where(
            lane_s < HEAD_DIM,
            summed,
            jnp.where(lane_s < 96, q, jnp.where(lane_s < 112, high, summed - high)),
        )
    for r in range(8):
        for oh in range(4):
            dh = lax.rem(g - oh + 4, 4)
            for dl in range(4):
                base = (r * 4 + oh) * 32 + dl * 2
                rows = [partial[pl.ds(base + k, 4, stride=8)] for k in range(2)]
                out_ref[r * 16 + dh * 4 + dl] = jnp.concatenate(rows, axis=0).astype(BF16)


def agent_kernel(
    returned_ref, live_ref, gain_ref, w_out, w_up, w_down_hbm, out_ref, w_down, w_sem
):
    w_copy = pltpu.make_async_copy(w_down_hbm, w_down, w_sem)
    w_copy.start()
    lane = iota((32, CH), 1)
    lower = lane < HEAD_DIM
    everything = returned_ref[...].astype(F32)
    attended = []
    embedded = []
    chunk_sum = None
    for h in range(HEADS):
        total = None
        for kp in range(4):
            chunk = h * 4 + kp
            block = everything[chunk * 4 : chunk * 4 + 4].reshape(32, CH)
            total = block if total is None else total + block
            whole = block + pltpu.roll(block, CH - 16, 1)
            placed = pltpu.roll(whole, (chunk % 8 * 16 - HEAD_DIM) % CH, 1)
            here = (lane // 16) == chunk % 8
            chunk_sum = jnp.where(here, placed, 0.0 if chunk % 8 == 0 else chunk_sum)
            if chunk % 8 == 7:
                embedded.append(chunk_sum)
        below = jnp.sum(jnp.where((lane == 96) | (lane == 112), total, 0.0), axis=1, keepdims=True)
        ratio = total / below
        if h % 2 == 0:
            even = ratio
        else:
            attended.append(jnp.where(lower, even, pltpu.roll(ratio, HEAD_DIM, 1)).astype(BF16))
    attended = jnp.concatenate(attended, axis=1)
    embedded = jnp.concatenate(embedded, axis=1)
    after = embedded + dot(attended, w_out[...])
    power = jnp.mean(after * after, axis=1, keepdims=True)
    normed = (after * lax.rsqrt(power + EPS) * gain_ref[...]).astype(BF16)
    activated = jax.nn.gelu(dot(normed, w_up[...])).astype(BF16)
    w_copy.wait()
    result = (after + dot(activated, w_down[...])).astype(BF16)
    dh = lax.axis_index("col") // 4
    slot = iota((32, 32), 0)
    at = iota((32, 32), 1)
    g = lax.rem(slot // 8 + dh, 4)
    place = g * 8 + lax.rem(slot, 2) * 4 + lax.rem(slot // 2, 4)
    order = (at == place).astype(F32).astype(BF16)
    out_ref[...] = (dot(order, result) * live_ref[...]).astype(BF16)


VMEM = pl.BlockSpec(memory_space=pltpu.VMEM)
SMEM = pl.BlockSpec(memory_space=pltpu.SMEM)
ANY = pl.BlockSpec(memory_space=pl.ANY)
HBM = pl.BlockSpec(memory_space=pltpu.HBM)


def first_layer(raster, above, below, conv1):
    return pl.pallas_call(
        first_kernel,
        out_shape=jax.ShapeDtypeStruct((2 * PAIRS_1, COLS, CH), BF16),
        in_specs=[HBM, ANY, ANY, VMEM],
        out_specs=HBM,
        scratch_shapes=[
            pltpu.VMEM((2 * SLOTS, COLS, CH), BF16),
            pltpu.VMEM((NB1 + 1, COLS, 4 * CH), BF16),
            pltpu.VMEM((NB1 + 1, COLS, 4 * CH), BF16),
            pltpu.VMEM((2 * NB1 + 2, 80, CH), F32),
            pltpu.VMEM((2 * PAIRS_1, COLS, CH), BF16),
            pltpu.VMEM((12 * CH, 2 * CH), BF16),
            pltpu.SemaphoreType.DMA((3,)),
            pltpu.SemaphoreType.DMA((PAIRS_1 // NB1,)),
        ],
        compiler_params=pltpu.CompilerParams(vmem_limit_bytes=32 * 2**20),
        cost_estimate=pl.CostEstimate(flops=4 * 10**9, bytes_accessed=5 * 10**6, transcendentals=0),
        name="first_layer",
    )(raster, above, below, conv1)


def scene(
    anchor, raster, above, below, left, right, inner, conv1, conv2, flags, gain, w_embed, w_qkv
):
    return pl.pallas_call(
        scene_kernel,
        out_shape=(
            jax.ShapeDtypeStruct((ROWS, COLS, CH), BF16),
            jax.ShapeDtypeStruct((128, 16, CH), BF16),
        ),
        in_specs=[SMEM, HBM, ANY, ANY, VMEM, VMEM, HBM, VMEM, VMEM, VMEM, VMEM, HBM, HBM],
        out_specs=(HBM, VMEM),
        scratch_shapes=[
            pltpu.VMEM((2 * SLOTS, COLS, CH), BF16),
            pltpu.VMEM((2 * PAIRS_1, COLS, CH), BF16),
            pltpu.VMEM((2 * SLOTS * 64, CH), F32),
            pltpu.VMEM((SLOTS, STRIP, 6 * CH), BF16),
            pltpu.VMEM((2 * PAIRS_1, STRIP, CH), F32),
            pltpu.VMEM((2 * NB2 + 2, 96, CH), F32),
            pltpu.VMEM((NB2 + 1, WIDE, 6 * CH), BF16),
            pltpu.VMEM((NB2 + 1, WIDE, 6 * CH), BF16),
            pltpu.VMEM((2 * PAIRS_2 * WIDE, CH), F32),
            pltpu.VMEM((2 * PAIRS_2, COLS, CH), BF16),
            pltpu.VMEM((12 * CH, 2 * CH), BF16),
            pltpu.VMEM((12 * CH, 2 * CH), BF16),
            pltpu.VMEM((4, CROP, CH), F32),
            pltpu.VMEM((16 * 32, CH), F32),
            pltpu.VMEM(w_embed.shape, BF16),
            pltpu.VMEM(w_qkv.shape, BF16),
            pltpu.SemaphoreType.DMA((4,)),
            pltpu.SemaphoreType.DMA((2,)),
            pltpu.SemaphoreType.DMA,
        ],
        compiler_params=pltpu.CompilerParams(vmem_limit_bytes=44 * 2**20),
        cost_estimate=pl.CostEstimate(flops=10**10, bytes_accessed=10**7, transcendentals=0),
        name="scene",
    )(
        anchor,
        raster,
        above,
        below,
        left,
        right,
        inner,
        conv1,
        conv2,
        flags,
        gain,
        w_embed,
        w_qkv,
    )


def attend(received):
    return pl.pallas_call(
        attend_kernel,
        out_shape=jax.ShapeDtypeStruct((128, 8, CH), BF16),
        in_specs=[VMEM],
        out_specs=VMEM,
        scratch_shapes=[pltpu.VMEM((1024, CH), F32), pltpu.VMEM((1024, CH), F32)],
        compiler_params=pltpu.CompilerParams(vmem_limit_bytes=24 * 2**20),
        name="attend",
    )(received)


def finish(returned, live, gain, w_out, w_up, w_down):
    return pl.pallas_call(
        agent_kernel,
        out_shape=jax.ShapeDtypeStruct((32, 512), BF16),
        in_specs=[VMEM] * 5 + [HBM],
        out_specs=VMEM,
        scratch_shapes=[pltpu.VMEM(w_down.shape, BF16), pltpu.SemaphoreType.DMA],
        compiler_params=pltpu.CompilerParams(vmem_limit_bytes=24 * 2**20),
        name="agents",
    )(returned, live, gain, w_out, w_up, w_down)


def per_device(
    raster,
    conv_first,
    conv_second,
    crop_anchor,
    agent_live,
    w_embed,
    gain_attn,
    w_qkv,
    w_out,
    gain_mlp,
    w_up,
    w_down,
):
    def forward(n):
        return [(i, i + 1) for i in range(n - 1)]

    def backward(n):
        return [(i + 1, i) for i in range(n - 1)]

    def plain(x):
        return with_layout_constraint(x, Layout(major_to_minor=(0, 1, 2)))

    below = plain(lax.ppermute(plain(raster[:FAR]), "row", backward(8)))
    above = plain(lax.ppermute(plain(raster[-NEAR:]), "row", forward(8)))
    parts = (above, raster, below)
    last = jnp.concatenate([p[:, -NEAR:].transpose(1, 0, 2) for p in parts], axis=1)
    initial = jnp.concatenate([p[:, :FAR].transpose(1, 0, 2) for p in parts], axis=1)
    right = lax.ppermute(initial, "col", backward(16))
    left = lax.ppermute(last, "col", forward(16))
    conv1 = conv_first.reshape(9, CH, CH)
    inner = first_layer(raster, above, below, conv1)
    flags = jnp.pad(agent_live.astype(F32)[None], ((0, 0), (96, 0)))
    features, payload = scene(
        crop_anchor,
        raster,
        above,
        below,
        left,
        right,
        inner,
        conv1,
        conv_second.reshape(9, CH, CH),
        flags,
        gain_attn[None],
        w_embed,
        w_qkv,
    )
    received = lax.all_to_all(payload, ("row", "col"), 0, 0, tiled=True)
    returned = lax.all_to_all(attend(received), ("row", "col"), 0, 0, tiled=True)
    live = agent_live.astype(F32)[:, None]
    agent_out = finish(returned, live, gain_mlp[None], w_out, w_up, w_down)
    return (features, agent_out)


def solution(mesh):
    in_specs = (
        P("row", "col", None),
        P(),
        P(),
        P(None, ("row", "col")),
        P(("row", "col")),
        P(),
        P(),
        P(),
        P(),
        P(),
        P(),
        P(),
    )
    out_specs = (P("row", "col", None), P(("row", "col"), None))
    return jax.shard_map(
        per_device, mesh=mesh, in_specs=in_specs, out_specs=out_specs, check_vma=False
    )
```

```python
import jax
import jax.numpy as jnp
from jax import lax
from jax.experimental import pallas as pl
from jax.experimental.pallas import tpu as pltpu
from jax.experimental.layout import Layout, with_layout_constraint
from jax.sharding import PartitionSpec as P

HEADS = 8
HEAD_DIM = 64
CROP = 16
EPS = 1e-06
SCORE_SCALE = 3.0

ROWS, COLS, CH = 128, 64, 128
NEAR, FAR = 2, 17
KNOWN = NEAR + ROWS + FAR
PAIRS_1 = 76
PAIRS_2 = 72
SLOTS = 77
NB1, NB2 = 19, 18
WIDE = 80
STRIP = 32
TAPS = ((0, 0), (0, 2), (1, 0), (1, 2), (0, 1), (1, 1))
F32, BF16 = jnp.float32, jnp.bfloat16


def dot(a, b):
    return lax.dot_general(a, b, (((1,), (0,)), ((), ())), preferred_element_type=F32)


def dot_t(a, b):
    return lax.dot_general(a, b, (((1,), (1,)), ((), ())), preferred_element_type=F32)


def iota(shape, dim):
    return lax.broadcasted_iota(jnp.int32, shape, dim)


def band(kernel_ref, band_ref):
    zero = jnp.zeros((CH, CH), BF16)
    for slot in range(2):
        for i, (par, b) in enumerate(TAPS):
            a = slot * 2 + par
            at = pl.ds((slot * 6 + i) * CH, CH)
            band_ref[at, 0:CH] = kernel_ref[a * 3 + b] if a < 3 else zero
            band_ref[at, CH : 2 * CH] = kernel_ref[(a - 1) * 3 + b] if a > 0 else zero


def rows_between(low, high, above_ref, raster_ref, below_ref):
    parts = []
    for ref, first, count in (
        (above_ref, 0, NEAR),
        (raster_ref, NEAR, ROWS),
        (below_ref, NEAR + ROWS, FAR),
    ):
        start, stop = max(low, first), min(high, first + count)
        if start < stop:
            parts.append(ref[start - first : stop - first])
    if high > KNOWN:
        parts.append(jnp.zeros((high - max(low, KNOWN), COLS, CH), BF16))
    return parts[0] if len(parts) == 1 else jnp.concatenate(parts, axis=0)


def row_inside(rho):
    return (rho >= 0) & (rho < ROWS * 8)


def slice_kernel(raster_hbm, top_ref, bottom_ref, sems):
    copies = [
        pltpu.make_async_copy(raster_hbm.at[pl.ds(0, FAR)], top_ref, sems.at[0]),
        pltpu.make_async_copy(raster_hbm.at[pl.ds(ROWS - NEAR, NEAR)], bottom_ref, sems.at[1]),
    ]
    for copy in copies:
        copy.start()
    for copy in copies:
        copy.wait()


def first_kernel(
    raster_ref,
    above_ref,
    below_ref,
    conv1_ref,
    inner_ref,
    shifted_a,
    shifted_b,
    row_wide,
    band_1,
):
    row_id = lax.axis_index("row")
    center = (above_ref, raster_ref, below_ref)
    band(conv1_ref, band_1)
    row_wide[:, 0:8] = jnp.zeros((2 * NB1 + 2, 8, CH), F32)
    row_wide[:, 72:80] = jnp.zeros((2 * NB1 + 2, 8, CH), F32)

    def spread(block, shifted):
        for i in range(NB1 + 1):
            for par in range(2):
                u = (block * NB1 + i) * 2 + par
                wide = row_wide.at[2 * i + par]
                wide[8:72] = rows_between(u, u + 1, *center)[0].astype(F32)
                shifted[i, :, (par * 2) * CH : (par * 2 + 1) * CH] = wide[7:71].astype(BF16)
                shifted[i, :, (par * 2 + 1) * CH : (par * 2 + 2) * CH] = wide[9:73].astype(BF16)

    def multiply(block, shifted):
        def side(s):
            u = (block * NB1 + s) * 2
            plain = rows_between(u, u + 2 * NB1, *center).reshape(NB1, 2, COLS, CH)
            parts = [shifted[s : s + NB1], plain[:, 0], plain[:, 1]]
            return jnp.concatenate(parts, axis=2).reshape(NB1 * COLS, 6 * CH)

        total = dot(side(0), band_1[0 : 6 * CH]) + dot(side(1), band_1[6 * CH :])
        total = jnp.maximum(total, 0.0)
        for i in range(NB1):
            for par in range(2):
                v = (block * NB1 + i) * 2 + par
                value = total[i * COLS : (i + 1) * COLS, par * CH : (par + 1) * CH]
                if v == 0 or v > ROWS:
                    value = jnp.where(row_inside(row_id * ROWS - 1 + v), value, 0.0)
                inner_ref[v] = value.astype(BF16)

    blocks = PAIRS_1 // NB1
    buffers = (shifted_a, shifted_b)
    spread(0, buffers[0])
    for block in range(blocks):
        multiply(block, buffers[block % 2])
        if block + 1 < blocks:
            spread(block + 1, buffers[(block + 1) % 2])


def scene_kernel(
    anchor_ref,
    raster_ref,
    above_ref,
    below_ref,
    left_ref,
    right_ref,
    inner_ref,
    conv1_ref,
    conv2_ref,
    flags_ref,
    gain_ref,
    w_embed,
    w_qkv,
    features_hbm,
    payload_ref,
    edge_wide,
    edge_a,
    edge_b,
    edge_first,
    row_first,
    shifted_a,
    shifted_b,
    wide_features,
    out_features,
    band_1,
    band_2,
    block_sum,
    pooled,
    out_sem,
):
    row_id = lax.axis_index("row")
    col_id = lax.axis_index("col")
    center = (above_ref, raster_ref, below_ref)
    band(conv1_ref, band_1)
    band(conv2_ref, band_2)
    for u in range(2 * SLOTS):
        edge_wide[u * 64 + 48 : u * 64 + 56] = jnp.zeros((8, CH), F32)
    for c in range(NEAR):
        edge_wide[pl.ds(6 + c, KNOWN, stride=64)] = left_ref[c].astype(F32)
    last = right_ref[KNOWN : KNOWN + 10].reshape(160, CH).astype(F32)
    edge_wide[pl.ds(48, KNOWN, stride=64)] = last[:KNOWN]

    def edges(block, shifted):
        for i in range(NB1 + 1):
            for par in range(2):
                u = (block * NB1 + i) * 2 + par
                if u < KNOWN:
                    row = rows_between(u, u + 1, *center)[0]
                    edge_wide[u * 64 + 8 : u * 64 + 16] = row[0:16].astype(F32)[0:8]
                    edge_wide[u * 64 + 24 : u * 64 + 32] = row[48:64].astype(F32)[8:16]
                    edge_wide[u * 64 + 32 : u * 64 + 48] = right_ref[u].astype(F32)
                else:
                    edge_wide[u * 64 : u * 64 + 56] = jnp.zeros((56, CH), F32)
            for k, (par, b) in enumerate(TAPS):
                at = ((block * NB1 + i) * 2 + par) * 64 + b
                both = jnp.concatenate(
                    [edge_wide[at + 6 : at + 14], edge_wide[at + 30 : at + 54]], axis=0
                )
                shifted[i, :, k * CH : (k + 1) * CH] = both.astype(BF16)

    strip = iota((STRIP, CH), 0)
    column = col_id * COLS + jnp.where(strip < 8, strip - 1, strip + 55)
    column_in = (column >= 0) & (column < COLS * 16)

    def edge_multiply(block, shifted):
        def side(s):
            return shifted[s : s + NB1].reshape(NB1 * STRIP, 6 * CH)

        total = dot(side(0), band_1[0 : 6 * CH]) + dot(side(1), band_1[6 * CH :])
        total = jnp.maximum(total, 0.0)
        for i in range(NB1):
            for par in range(2):
                v = (block * NB1 + i) * 2 + par
                value = total[i * STRIP : (i + 1) * STRIP, par * CH : (par + 1) * CH]
                keep = column_in
                if v == 0 or v > ROWS:
                    keep = keep & row_inside(row_id * ROWS - 1 + v)
                edge_first[v] = jnp.where(keep, value, 0.0)

    def assemble(block, shifted):
        for i in range(NB2 + 1):
            for par in range(2):
                v = (block * NB2 + i) * 2 + par
                first = row_first.at[2 * i + par]
                first[8:72] = inner_ref[v].astype(F32)
                first[7:9] = edge_first[v, 0:2]
                first[71:95] = edge_first[v, 8:32]
            for k, (par, b) in enumerate(TAPS):
                window = row_first[2 * i + par, 7 + b : 7 + b + WIDE]
                shifted[i, :, k * CH : (k + 1) * CH] = window.astype(BF16)

    def multiply(block, shifted):
        def side(s):
            return shifted[s : s + NB2].reshape(NB2 * WIDE, 6 * CH)

        total = dot(side(0), band_2[0 : 6 * CH]) + dot(side(1), band_2[6 * CH :])
        for i in range(NB2):
            for par in range(2):
                row = (block * NB2 + i) * 2 + par
                u = row + NEAR
                middle = rows_between(u, u + 1, *center)[0].astype(F32)
                base = jnp.concatenate([middle, right_ref[u].astype(F32)], axis=0)
                value = total[i * WIDE : (i + 1) * WIDE, par * CH : (par + 1) * CH] + base
                value = value.astype(BF16)
                wide_features[row * WIDE : (row + 1) * WIDE] = value.astype(F32)
                out_features[row] = value[:COLS]

    blocks = PAIRS_1 // NB1
    buffers = (edge_a, edge_b)
    edges(0, buffers[0])
    for block in range(blocks):
        edge_multiply(block, buffers[block % 2])
        if block + 1 < blocks:
            edges(block + 1, buffers[(block + 1) % 2])
    blocks = PAIRS_2 // NB2
    buffers = (shifted_a, shifted_b)
    assemble(0, buffers[0])
    for block in range(blocks):
        multiply(block, buffers[block % 2])
        if block + 1 < blocks:
            assemble(block + 1, buffers[(block + 1) % 2])
    out_copy = pltpu.make_async_copy(out_features.at[pl.ds(0, ROWS)], features_hbm, out_sem)
    out_copy.start()

    def crop(agent, _):
        top = anchor_ref[0, agent] - row_id * ROWS
        left = anchor_ref[1, agent] - col_id * COLS
        for rb in range(4):
            start = (top + rb * 4) * WIDE + left
            four = [wide_features[pl.ds(start + i * WIDE, CROP)] for i in range(4)]
            block_sum[rb] = (four[0] + four[1]) + (four[2] + four[3])
        for rb in range(4):
            cells = [block_sum[rb, pl.ds(k, 4, stride=4)] for k in range(4)]
            mean = ((cells[0] + cells[1]) + (cells[2] + cells[3])) * (1.0 / 16)
            pooled[pl.ds(rb * 4 * 32 + agent, 4, stride=32)] = mean
        return _

    lax.fori_loop(0, 32, crop, 0)
    agents = jnp.concatenate(
        [pooled[b * 32 : (b + 1) * 32].astype(BF16) for b in range(16)], axis=1
    )
    embedded = dot(agents, w_embed[...])
    power = jnp.mean(embedded * embedded, axis=1, keepdims=True)
    normed = (embedded * lax.rsqrt(power + EPS) * gain_ref[...]).astype(BF16)
    projected = dot(normed, w_qkv[...])
    lane_id = iota((32, CH), 1)
    lower = lane_id < HEAD_DIM

    def unit(x):
        squared = x * x
        first_half = jnp.sum(jnp.where(lower, squared, 0.0), axis=1, keepdims=True)
        second_half = jnp.sum(jnp.where(lower, 0.0, squared), axis=1, keepdims=True)
        scale = lax.rsqrt(jnp.where(lower, first_half, second_half) * (1.0 / HEAD_DIM) + EPS)
        return x * scale

    def turned(x):
        return pltpu.roll(x, HEAD_DIM, 1)

    shift = lax.rem(col_id // 4, 4)
    for pair in range(4):
        q_two = unit(projected[:, pair * CH : (pair + 1) * CH])
        k_two = unit(projected[:, 512 + pair * CH : 512 + (pair + 1) * CH])
        v_two = projected[:, 1024 + pair * CH : 1024 + (pair + 1) * CH]
        rolled = (turned(q_two), turned(k_two), turned(v_two))
        for half in range(2):
            h = pair * 2 + half
            q_h = rolled[0] if half else q_two
            k_h = rolled[1] if half else k_two
            v_h = v_two if half else rolled[2]
            kv = jnp.where(lower, k_h, v_h)
            for kp in range(4):
                chunk = h * 4 + kp
                source = embedded[:, (chunk // 8) * CH : (chunk // 8 + 1) * CH]
                offset = (chunk % 8) * 16
                piece = pltpu.roll(source, (HEAD_DIM - offset) % CH, 1)
                high = piece.astype(BF16).astype(F32)
                low = pltpu.roll(piece - high, 16, 1)
                extra = jnp.where(
                    lane_id < 80, high, jnp.where(lane_id < 96, low, flags_ref[...])
                )
                row = jnp.where(lower, q_h, extra)
                for gg in range(4):
                    g = lax.rem(gg + shift, 4)
                    both = jnp.concatenate(
                        [kv[kp * 8 : kp * 8 + 8], row[gg * 8 : gg * 8 + 8]], axis=0
                    )
                    payload_ref[chunk * 4 + g] = both.astype(BF16)
    out_copy.wait()


def attend_kernel(received_ref, w_down_hbm, out_ref, w_down_ref, queries, partial, w_sem):
    w_copy = pltpu.make_async_copy(w_down_hbm, w_down_ref, w_sem)
    w_copy.start()
    device = lax.axis_index("row") * 16 + lax.axis_index("col")
    quarter = lax.rem(device // 4, 4)
    g = lax.rem(device, 4)
    everything = received_ref[...].astype(F32)
    kv = everything[:, 0:8].reshape(1024, CH)
    q_rows = everything[:, 8:16].reshape(1024, CH)
    queries[...] = q_rows
    flags = queries[pl.ds(0, 128, stride=8)].astype(BF16)
    key = iota((1024, CH), 0)
    lane = iota((1024, CH), 1)
    source = (key // 128) * 16 + quarter * 4 + lax.rem(key // 2, 4)
    chosen = dot((lane == source).astype(F32).astype(BF16), flags)
    wanted = 96 + lax.rem(key // 8, 16) * 2 + lax.rem(key, 2)
    alone = jnp.where(lane == wanted, chosen, 0.0).astype(BF16)
    mask = dot(alone, jnp.ones((CH, CH), BF16))
    lower = lane < HEAD_DIM
    keys = jnp.where(lower, kv, 0.0).astype(BF16)
    values = (jnp.where(lower, 1.0, kv) * mask).astype(BF16)
    factor = SCORE_SCALE / HEAD_DIM**0.5
    step = 256
    lane_s = iota((step, CH), 1)
    for i in range(1024 // step):
        q = queries[i * step : (i + 1) * step]
        weights = jnp.exp(dot_t(q.astype(BF16), keys) * factor).astype(BF16)
        summed = pltpu.roll(dot(weights, values), HEAD_DIM, 1)
        high = summed.astype(BF16).astype(F32)
        partial[i * step : (i + 1) * step] = jnp.where(
            lane_s < HEAD_DIM,
            summed,
            jnp.where(lane_s < 96, q, jnp.where(lane_s < 112, high, summed - high)),
        )
    for r in range(8):
        for oh in range(4):
            dh = lax.rem(g - oh + 4, 4)
            for dl in range(4):
                base = (r * 4 + oh) * 32 + dl * 2
                rows = [partial[pl.ds(base + k, 4, stride=8)] for k in range(2)]
                out_ref[r * 16 + dh * 4 + dl] = jnp.concatenate(rows, axis=0).astype(BF16)
    w_copy.wait()


def agent_kernel(returned_ref, live_ref, gain_ref, w_out, w_up, w_down, out_ref):
    lane = iota((32, CH), 1)
    lower = lane < HEAD_DIM
    everything = returned_ref[...].astype(F32)
    attended = []
    embedded = []
    chunk_sum = None
    for h in range(HEADS):
        total = None
        for kp in range(4):
            chunk = h * 4 + kp
            block = everything[chunk * 4 : chunk * 4 + 4].reshape(32, CH)
            total = block if total is None else total + block
            whole = block + pltpu.roll(block, CH - 16, 1)
            placed = pltpu.roll(whole, (chunk % 8 * 16 - HEAD_DIM) % CH, 1)
            here = (lane // 16) == chunk % 8
            chunk_sum = jnp.where(here, placed, 0.0 if chunk % 8 == 0 else chunk_sum)
            if chunk % 8 == 7:
                embedded.append(chunk_sum)
        below = jnp.sum(jnp.where((lane == 96) | (lane == 112), total, 0.0), axis=1, keepdims=True)
        ratio = total / below
        if h % 2 == 0:
            even = ratio
        else:
            attended.append(jnp.where(lower, even, pltpu.roll(ratio, HEAD_DIM, 1)).astype(BF16))
    attended = jnp.concatenate(attended, axis=1)
    embedded = jnp.concatenate(embedded, axis=1)
    after = embedded + dot(attended, w_out[...])
    power = jnp.mean(after * after, axis=1, keepdims=True)
    normed = (after * lax.rsqrt(power + EPS) * gain_ref[...]).astype(BF16)
    activated = jax.nn.gelu(dot(normed, w_up[...])).astype(BF16)
    result = (after + dot(activated, w_down[...])).astype(BF16)
    dh = lax.axis_index("col") // 4
    slot = iota((32, 32), 0)
    at = iota((32, 32), 1)
    g = lax.rem(slot // 8 + dh, 4)
    place = g * 8 + lax.rem(slot, 2) * 4 + lax.rem(slot // 2, 4)
    order = (at == place).astype(F32).astype(BF16)
    out_ref[...] = (dot(order, result) * live_ref[...]).astype(BF16)


VMEM = pl.BlockSpec(memory_space=pltpu.VMEM)
SMEM = pl.BlockSpec(memory_space=pltpu.SMEM)
HBM = pl.BlockSpec(memory_space=pltpu.HBM)


def row_slices(raster):
    return pl.pallas_call(
        slice_kernel,
        out_shape=(
            jax.ShapeDtypeStruct((FAR, COLS, CH), BF16),
            jax.ShapeDtypeStruct((NEAR, COLS, CH), BF16),
        ),
        in_specs=[HBM],
        out_specs=(VMEM, VMEM),
        scratch_shapes=[pltpu.SemaphoreType.DMA((2,))],
        name="row_slices",
    )(raster)


def first_layer(raster, above, below, conv1):
    return pl.pallas_call(
        first_kernel,
        out_shape=jax.ShapeDtypeStruct((2 * PAIRS_1, COLS, CH), BF16),
        in_specs=[VMEM] * 4,
        out_specs=VMEM,
        scratch_shapes=[
            pltpu.VMEM((NB1 + 1, COLS, 4 * CH), BF16),
            pltpu.VMEM((NB1 + 1, COLS, 4 * CH), BF16),
            pltpu.VMEM((2 * NB1 + 2, 80, CH), F32),
            pltpu.VMEM((12 * CH, 2 * CH), BF16),
        ],
        compiler_params=pltpu.CompilerParams(vmem_limit_bytes=32 * 2**20),
        cost_estimate=pl.CostEstimate(flops=4 * 10**9, bytes_accessed=5 * 10**6, transcendentals=0),
        name="first_layer",
    )(raster, above, below, conv1)


def scene(
    anchor, raster, above, below, left, right, inner, conv1, conv2, flags, gain, w_embed, w_qkv
):
    return pl.pallas_call(
        scene_kernel,
        out_shape=(
            jax.ShapeDtypeStruct((ROWS, COLS, CH), BF16),
            jax.ShapeDtypeStruct((128, 16, CH), BF16),
        ),
        in_specs=[SMEM] + [VMEM] * 12,
        out_specs=(HBM, VMEM),
        scratch_shapes=[
            pltpu.VMEM((2 * SLOTS * 64, CH), F32),
            pltpu.VMEM((NB1 + 1, STRIP, 6 * CH), BF16),
            pltpu.VMEM((NB1 + 1, STRIP, 6 * CH), BF16),
            pltpu.VMEM((2 * PAIRS_1, STRIP, CH), F32),
            pltpu.VMEM((2 * NB2 + 2, 96, CH), F32),
            pltpu.VMEM((NB2 + 1, WIDE, 6 * CH), BF16),
            pltpu.VMEM((NB2 + 1, WIDE, 6 * CH), BF16),
            pltpu.VMEM((2 * PAIRS_2 * WIDE, CH), F32),
            pltpu.VMEM((2 * PAIRS_2, COLS, CH), BF16),
            pltpu.VMEM((12 * CH, 2 * CH), BF16),
            pltpu.VMEM((12 * CH, 2 * CH), BF16),
            pltpu.VMEM((4, CROP, CH), F32),
            pltpu.VMEM((16 * 32, CH), F32),
            pltpu.SemaphoreType.DMA,
        ],
        compiler_params=pltpu.CompilerParams(vmem_limit_bytes=44 * 2**20),
        cost_estimate=pl.CostEstimate(flops=10**10, bytes_accessed=10**7, transcendentals=0),
        name="scene",
    )(
        anchor,
        raster,
        above,
        below,
        left,
        right,
        inner,
        conv1,
        conv2,
        flags,
        gain,
        w_embed,
        w_qkv,
    )


def attend(received, w_down):
    return pl.pallas_call(
        attend_kernel,
        out_shape=(
            jax.ShapeDtypeStruct((128, 8, CH), BF16),
            jax.ShapeDtypeStruct(w_down.shape, BF16),
        ),
        in_specs=[VMEM, HBM],
        out_specs=(VMEM, VMEM),
        scratch_shapes=[
            pltpu.VMEM((1024, CH), F32),
            pltpu.VMEM((1024, CH), F32),
            pltpu.SemaphoreType.DMA,
        ],
        compiler_params=pltpu.CompilerParams(vmem_limit_bytes=24 * 2**20),
        cost_estimate=pl.CostEstimate(
            flops=10**9, bytes_accessed=10**6, transcendentals=2 * 10**6
        ),
        name="attend",
    )(received, w_down)


def finish(returned, live, gain, w_out, w_up, w_down):
    return pl.pallas_call(
        agent_kernel,
        out_shape=jax.ShapeDtypeStruct((32, 512), BF16),
        in_specs=[VMEM] * 6,
        out_specs=VMEM,
        compiler_params=pltpu.CompilerParams(vmem_limit_bytes=24 * 2**20),
        name="agents",
    )(returned, live, gain, w_out, w_up, w_down)


def per_device(
    raster,
    conv_first,
    conv_second,
    crop_anchor,
    agent_live,
    w_embed,
    gain_attn,
    w_qkv,
    w_out,
    gain_mlp,
    w_up,
    w_down,
):
    def forward(n):
        return [(i, i + 1) for i in range(n - 1)]

    def backward(n):
        return [(i + 1, i) for i in range(n - 1)]

    def plain(x):
        return with_layout_constraint(x, Layout(major_to_minor=(0, 1, 2)))

    top, bottom = row_slices(raster)
    below = plain(lax.ppermute(top, "row", backward(8)))
    above = plain(lax.ppermute(bottom, "row", forward(8)))
    parts = (above, raster, below)
    last = jnp.concatenate([p[:, -NEAR:].transpose(1, 0, 2) for p in parts], axis=1)
    extra = jnp.concatenate([p[:, FAR - 1] for p in parts], axis=0)
    extra = jnp.pad(extra, ((0, 160 - KNOWN), (0, 0))).reshape(10, 16, CH)
    initial = jnp.concatenate([p[:, : FAR - 1] for p in parts] + [extra], axis=0)
    right = plain(lax.ppermute(plain(initial), "col", backward(16)))
    left = lax.ppermute(last, "col", forward(16))
    conv1 = conv_first.reshape(9, CH, CH)
    inner = first_layer(raster, above, below, conv1)
    flags = jnp.pad(agent_live.astype(F32)[None], ((0, 0), (96, 0)))
    features, payload = scene(
        crop_anchor,
        raster,
        above,
        below,
        left,
        right,
        inner,
        conv1,
        conv_second.reshape(9, CH, CH),
        flags,
        gain_attn[None],
        w_embed,
        w_qkv,
    )
    received = lax.all_to_all(payload, ("row", "col"), 0, 0, tiled=True)
    partial, w_down = attend(received, w_down)
    returned = lax.all_to_all(partial, ("row", "col"), 0, 0, tiled=True)
    live = agent_live.astype(F32)[:, None]
    agent_out = finish(returned, live, gain_mlp[None], w_out, w_up, w_down)
    return (features, agent_out)


def solution(mesh):
    in_specs = (
        P("row", "col", None),
        P(),
        P(),
        P(None, ("row", "col")),
        P(("row", "col")),
        P(),
        P(),
        P(),
        P(),
        P(),
        P(),
        P(),
    )
    out_specs = (P("row", "col", None), P(("row", "col"), None))
    return jax.shard_map(
        per_device, mesh=mesh, in_specs=in_specs, out_specs=out_specs, check_vma=False
    )
```

```python
import jax
import jax.numpy as jnp
from jax import lax
from jax.experimental import pallas as pl
from jax.experimental.pallas import tpu as pltpu
from jax.experimental.layout import Layout, with_layout_constraint
from jax.sharding import PartitionSpec as P

HEADS = 8
HEAD_DIM = 64
CROP = 16
EPS = 1e-06
SCORE_SCALE = 3.0

ROWS, COLS, CH = 128, 64, 128
NEAR, FAR = 2, 17
KNOWN = NEAR + ROWS + FAR
PAIRS_1 = 76
PAIRS_2 = 72
SLOTS = 77
NB1, NB2 = 19, 18
WIDE = 80
STRIP = 32
TAPS = ((0, 0), (0, 2), (1, 0), (1, 2), (0, 1), (1, 1))
F32, BF16 = jnp.float32, jnp.bfloat16


def dot(a, b):
    return lax.dot_general(a, b, (((1,), (0,)), ((), ())), preferred_element_type=F32)


def dot_t(a, b):
    return lax.dot_general(a, b, (((1,), (1,)), ((), ())), preferred_element_type=F32)


def iota(shape, dim):
    return lax.broadcasted_iota(jnp.int32, shape, dim)


def band(kernel_ref, band_ref):
    zero = jnp.zeros((CH, CH), BF16)
    for slot in range(2):
        for i, (par, b) in enumerate(TAPS):
            a = slot * 2 + par
            at = pl.ds((slot * 6 + i) * CH, CH)
            band_ref[at, 0:CH] = kernel_ref[a * 3 + b] if a < 3 else zero
            band_ref[at, CH : 2 * CH] = kernel_ref[(a - 1) * 3 + b] if a > 0 else zero


def rows_between(low, high, above_ref, raster_ref, below_ref):
    parts = []
    for ref, first, count in (
        (above_ref, 0, NEAR),
        (raster_ref, NEAR, ROWS),
        (below_ref, NEAR + ROWS, FAR),
    ):
        start, stop = max(low, first), min(high, first + count)
        if start < stop:
            parts.append(ref[start - first : stop - first])
    if high > KNOWN:
        parts.append(jnp.zeros((high - max(low, KNOWN), COLS, CH), BF16))
    return parts[0] if len(parts) == 1 else jnp.concatenate(parts, axis=0)


def row_inside(rho):
    return (rho >= 0) & (rho < ROWS * 8)


def slice_kernel(raster_hbm, top_ref, bottom_ref, sems):
    copies = [
        pltpu.make_async_copy(raster_hbm.at[pl.ds(0, FAR)], top_ref, sems.at[0]),
        pltpu.make_async_copy(raster_hbm.at[pl.ds(ROWS - NEAR, NEAR)], bottom_ref, sems.at[1]),
    ]
    for copy in copies:
        copy.start()
    for copy in copies:
        copy.wait()


def first_kernel(
    raster_ref,
    above_ref,
    below_ref,
    conv1_ref,
    inner_ref,
    shifted_a,
    shifted_b,
    row_wide,
    band_1,
):
    row_id = lax.axis_index("row")
    center = (above_ref, raster_ref, below_ref)
    band(conv1_ref, band_1)
    row_wide[:, 0:8] = jnp.zeros((2 * NB1 + 2, 8, CH), F32)
    row_wide[:, 72:80] = jnp.zeros((2 * NB1 + 2, 8, CH), F32)

    def spread(block, shifted):
        for i in range(NB1 + 1):
            for par in range(2):
                u = (block * NB1 + i) * 2 + par
                wide = row_wide.at[2 * i + par]
                wide[8:72] = rows_between(u, u + 1, *center)[0].astype(F32)
                shifted[i, :, (par * 2) * CH : (par * 2 + 1) * CH] = wide[7:71].astype(BF16)
                shifted[i, :, (par * 2 + 1) * CH : (par * 2 + 2) * CH] = wide[9:73].astype(BF16)

    def multiply(block, shifted):
        def side(s):
            u = (block * NB1 + s) * 2
            plain = rows_between(u, u + 2 * NB1, *center).reshape(NB1, 2, COLS, CH)
            parts = [shifted[s : s + NB1], plain[:, 0], plain[:, 1]]
            return jnp.concatenate(parts, axis=2).reshape(NB1 * COLS, 6 * CH)

        total = dot(side(0), band_1[0 : 6 * CH]) + dot(side(1), band_1[6 * CH :])
        total = jnp.maximum(total, 0.0)
        for i in range(NB1):
            for par in range(2):
                v = (block * NB1 + i) * 2 + par
                value = total[i * COLS : (i + 1) * COLS, par * CH : (par + 1) * CH]
                if v == 0 or v > ROWS:
                    value = jnp.where(row_inside(row_id * ROWS - 1 + v), value, 0.0)
                inner_ref[v] = value.astype(BF16)

    blocks = PAIRS_1 // NB1
    buffers = (shifted_a, shifted_b)
    spread(0, buffers[0])
    for block in range(blocks):
        multiply(block, buffers[block % 2])
        if block + 1 < blocks:
            spread(block + 1, buffers[(block + 1) % 2])


def scene_kernel(
    anchor_ref,
    raster_ref,
    above_ref,
    below_ref,
    left_ref,
    right_ref,
    inner_ref,
    conv1_ref,
    conv2_ref,
    flags_ref,
    gain_ref,
    w_embed,
    w_qkv,
    features_hbm,
    payload_ref,
    edge_wide,
    edge_a,
    edge_b,
    edge_first,
    row_first,
    shifted_a,
    shifted_b,
    wide_features,
    out_features,
    band_1,
    band_2,
    block_sum,
    pooled,
    out_sem,
):
    row_id = lax.axis_index("row")
    col_id = lax.axis_index("col")
    center = (above_ref, raster_ref, below_ref)
    band(conv1_ref, band_1)
    band(conv2_ref, band_2)
    for u in range(2 * SLOTS):
        edge_wide[u * 64 + 48 : u * 64 + 56] = jnp.zeros((8, CH), F32)
    for c in range(NEAR):
        edge_wide[pl.ds(6 + c, KNOWN, stride=64)] = left_ref[c].astype(F32)
    last = right_ref[KNOWN : KNOWN + 10].reshape(160, CH).astype(F32)
    edge_wide[pl.ds(48, KNOWN, stride=64)] = last[:KNOWN]

    def edges(block, shifted):
        for i in range(NB1 + 1):
            for par in range(2):
                u = (block * NB1 + i) * 2 + par
                if u < KNOWN:
                    row = rows_between(u, u + 1, *center)[0]
                    edge_wide[u * 64 + 8 : u * 64 + 16] = row[0:16].astype(F32)[0:8]
                    edge_wide[u * 64 + 24 : u * 64 + 32] = row[48:64].astype(F32)[8:16]
                    edge_wide[u * 64 + 32 : u * 64 + 48] = right_ref[u].astype(F32)
                else:
                    edge_wide[u * 64 : u * 64 + 56] = jnp.zeros((56, CH), F32)
            for k, (par, b) in enumerate(TAPS):
                at = ((block * NB1 + i) * 2 + par) * 64 + b
                both = jnp.concatenate(
                    [edge_wide[at + 6 : at + 14], edge_wide[at + 30 : at + 54]], axis=0
                )
                shifted[i, :, k * CH : (k + 1) * CH] = both.astype(BF16)

    strip = iota((STRIP, CH), 0)
    column = col_id * COLS + jnp.where(strip < 8, strip - 1, strip + 55)
    column_in = (column >= 0) & (column < COLS * 16)

    def edge_multiply(block, shifted):
        def side(s):
            return shifted[s : s + NB1].reshape(NB1 * STRIP, 6 * CH)

        total = dot(side(0), band_1[0 : 6 * CH]) + dot(side(1), band_1[6 * CH :])
        total = jnp.maximum(total, 0.0)
        for i in range(NB1):
            for par in range(2):
                v = (block * NB1 + i) * 2 + par
                value = total[i * STRIP : (i + 1) * STRIP, par * CH : (par + 1) * CH]
                keep = column_in
                if v == 0 or v > ROWS:
                    keep = keep & row_inside(row_id * ROWS - 1 + v)
                edge_first[v] = jnp.where(keep, value, 0.0)

    def assemble(block, shifted):
        for i in range(NB2 + 1):
            for par in range(2):
                v = (block * NB2 + i) * 2 + par
                first = row_first.at[2 * i + par]
                first[8:72] = inner_ref[v].astype(F32)
                first[7:9] = edge_first[v, 0:2]
                first[71:95] = edge_first[v, 8:32]
            for k, (par, b) in enumerate(TAPS):
                window = row_first[2 * i + par, 7 + b : 7 + b + WIDE]
                shifted[i, :, k * CH : (k + 1) * CH] = window.astype(BF16)

    def multiply(block, shifted):
        def side(s):
            return shifted[s : s + NB2].reshape(NB2 * WIDE, 6 * CH)

        total = dot(side(0), band_2[0 : 6 * CH]) + dot(side(1), band_2[6 * CH :])
        for i in range(NB2):
            for par in range(2):
                row = (block * NB2 + i) * 2 + par
                u = row + NEAR
                middle = rows_between(u, u + 1, *center)[0].astype(F32)
                base = jnp.concatenate([middle, right_ref[u].astype(F32)], axis=0)
                value = total[i * WIDE : (i + 1) * WIDE, par * CH : (par + 1) * CH] + base
                value = value.astype(BF16)
                wide_features[row * WIDE : (row + 1) * WIDE] = value.astype(F32)
                out_features[row] = value[:COLS]

    blocks = PAIRS_1 // NB1
    buffers = (edge_a, edge_b)
    edges(0, buffers[0])
    for block in range(blocks):
        edge_multiply(block, buffers[block % 2])
        if block + 1 < blocks:
            edges(block + 1, buffers[(block + 1) % 2])
    blocks = PAIRS_2 // NB2
    buffers = (shifted_a, shifted_b)
    assemble(0, buffers[0])
    for block in range(blocks):
        multiply(block, buffers[block % 2])
        if block + 1 < blocks:
            assemble(block + 1, buffers[(block + 1) % 2])
    out_copy = pltpu.make_async_copy(out_features.at[pl.ds(0, ROWS)], features_hbm, out_sem)
    out_copy.start()

    def crop(agent, _):
        top = anchor_ref[0, agent] - row_id * ROWS
        left = anchor_ref[1, agent] - col_id * COLS
        for rb in range(4):
            start = (top + rb * 4) * WIDE + left
            four = [wide_features[pl.ds(start + i * WIDE, CROP)] for i in range(4)]
            block_sum[rb] = (four[0] + four[1]) + (four[2] + four[3])
        for rb in range(4):
            cells = [block_sum[rb, pl.ds(k, 4, stride=4)] for k in range(4)]
            mean = ((cells[0] + cells[1]) + (cells[2] + cells[3])) * (1.0 / 16)
            pooled[pl.ds(rb * 4 * 32 + agent, 4, stride=32)] = mean
        return _

    lax.fori_loop(0, 32, crop, 0)
    agents = jnp.concatenate(
        [pooled[b * 32 : (b + 1) * 32].astype(BF16) for b in range(16)], axis=1
    )
    embedded = dot(agents, w_embed[...])
    power = jnp.mean(embedded * embedded, axis=1, keepdims=True)
    normed = (embedded * lax.rsqrt(power + EPS) * gain_ref[...]).astype(BF16)
    projected = dot(normed, w_qkv[...])
    lane_id = iota((32, CH), 1)
    lower = lane_id < HEAD_DIM

    def unit(x):
        squared = x * x
        first_half = jnp.sum(jnp.where(lower, squared, 0.0), axis=1, keepdims=True)
        second_half = jnp.sum(jnp.where(lower, 0.0, squared), axis=1, keepdims=True)
        scale = lax.rsqrt(jnp.where(lower, first_half, second_half) * (1.0 / HEAD_DIM) + EPS)
        return x * scale

    def turned(x):
        return pltpu.roll(x, HEAD_DIM, 1)

    shift = lax.rem(col_id // 4, 4)
    for pair in range(4):
        q_two = unit(projected[:, pair * CH : (pair + 1) * CH])
        k_two = unit(projected[:, 512 + pair * CH : 512 + (pair + 1) * CH])
        v_two = projected[:, 1024 + pair * CH : 1024 + (pair + 1) * CH]
        rolled = (turned(q_two), turned(k_two), turned(v_two))
        for half in range(2):
            h = pair * 2 + half
            q_h = rolled[0] if half else q_two
            k_h = rolled[1] if half else k_two
            v_h = v_two if half else rolled[2]
            kv = jnp.where(lower, k_h, v_h)
            for kp in range(4):
                chunk = h * 4 + kp
                source = embedded[:, (chunk // 8) * CH : (chunk // 8 + 1) * CH]
                offset = (chunk % 8) * 16
                piece = pltpu.roll(source, (HEAD_DIM - offset) % CH, 1)
                high = piece.astype(BF16).astype(F32)
                low = pltpu.roll(piece - high, 16, 1)
                extra = jnp.where(
                    lane_id < 80, high, jnp.where(lane_id < 96, low, flags_ref[...])
                )
                row = jnp.where(lower, q_h, extra)
                for gg in range(4):
                    g = lax.rem(gg + shift, 4)
                    both = jnp.concatenate(
                        [kv[kp * 8 : kp * 8 + 8], row[gg * 8 : gg * 8 + 8]], axis=0
                    )
                    payload_ref[chunk * 4 + g] = both.astype(BF16)
    out_copy.wait()


def attend_kernel(received_ref, out_ref, queries, partial):
    device = lax.axis_index("row") * 16 + lax.axis_index("col")
    quarter = lax.rem(device // 4, 4)
    g = lax.rem(device, 4)
    everything = received_ref[...].astype(F32)
    kv = everything[:, 0:8].reshape(1024, CH)
    q_rows = everything[:, 8:16].reshape(1024, CH)
    queries[...] = q_rows
    flags = queries[pl.ds(0, 128, stride=8)].astype(BF16)
    key = iota((1024, CH), 0)
    lane = iota((1024, CH), 1)
    source = (key // 128) * 16 + quarter * 4 + lax.rem(key // 2, 4)
    chosen = dot((lane == source).astype(F32).astype(BF16), flags)
    wanted = 96 + lax.rem(key // 8, 16) * 2 + lax.rem(key, 2)
    alone = jnp.where(lane == wanted, chosen, 0.0).astype(BF16)
    mask = dot(alone, jnp.ones((CH, CH), BF16))
    lower = lane < HEAD_DIM
    keys = jnp.where(lower, kv, 0.0).astype(BF16)
    values = (jnp.where(lower, 1.0, kv) * mask).astype(BF16)
    factor = SCORE_SCALE / HEAD_DIM**0.5
    step = 256
    lane_s = iota((step, CH), 1)
    for i in range(1024 // step):
        q = queries[i * step : (i + 1) * step]
        weights = jnp.exp(dot_t(q.astype(BF16), keys) * factor).astype(BF16)
        summed = pltpu.roll(dot(weights, values), HEAD_DIM, 1)
        high = summed.astype(BF16).astype(F32)
        partial[i * step : (i + 1) * step] = jnp.where(
            lane_s < HEAD_DIM,
            summed,
            jnp.where(lane_s < 96, q, jnp.where(lane_s < 112, high, summed - high)),
        )
    for r in range(8):
        for oh in range(4):
            dh = lax.rem(g - oh + 4, 4)
            for dl in range(4):
                base = (r * 4 + oh) * 32 + dl * 2
                rows = [partial[pl.ds(base + k, 4, stride=8)] for k in range(2)]
                out_ref[r * 16 + dh * 4 + dl] = jnp.concatenate(rows, axis=0).astype(BF16)


def agent_kernel(
    returned_ref, live_ref, gain_ref, w_out, w_up, w_down_hbm, out_ref, w_down, w_sem
):
    w_copy = pltpu.make_async_copy(w_down_hbm, w_down, w_sem)
    w_copy.start()
    lane = iota((32, CH), 1)
    lower = lane < HEAD_DIM
    everything = returned_ref[...].astype(F32)
    attended = []
    embedded = []
    chunk_sum = None
    for h in range(HEADS):
        total = None
        for kp in range(4):
            chunk = h * 4 + kp
            block = everything[chunk * 4 : chunk * 4 + 4].reshape(32, CH)
            total = block if total is None else total + block
            whole = block + pltpu.roll(block, CH - 16, 1)
            placed = pltpu.roll(whole, (chunk % 8 * 16 - HEAD_DIM) % CH, 1)
            here = (lane // 16) == chunk % 8
            chunk_sum = jnp.where(here, placed, 0.0 if chunk % 8 == 0 else chunk_sum)
            if chunk % 8 == 7:
                embedded.append(chunk_sum)
        below = jnp.sum(jnp.where((lane == 96) | (lane == 112), total, 0.0), axis=1, keepdims=True)
        ratio = total / below
        if h % 2 == 0:
            even = ratio
        else:
            attended.append(jnp.where(lower, even, pltpu.roll(ratio, HEAD_DIM, 1)).astype(BF16))
    attended = jnp.concatenate(attended, axis=1)
    embedded = jnp.concatenate(embedded, axis=1)
    after = embedded + dot(attended, w_out[...])
    power = jnp.mean(after * after, axis=1, keepdims=True)
    normed = (after * lax.rsqrt(power + EPS) * gain_ref[...]).astype(BF16)
    activated = jax.nn.gelu(dot(normed, w_up[...])).astype(BF16)
    w_copy.wait()
    result = (after + dot(activated, w_down[...])).astype(BF16)
    dh = lax.axis_index("col") // 4
    slot = iota((32, 32), 0)
    at = iota((32, 32), 1)
    g = lax.rem(slot // 8 + dh, 4)
    place = g * 8 + lax.rem(slot, 2) * 4 + lax.rem(slot // 2, 4)
    order = (at == place).astype(F32).astype(BF16)
    out_ref[...] = (dot(order, result) * live_ref[...]).astype(BF16)


VMEM = pl.BlockSpec(memory_space=pltpu.VMEM)
SMEM = pl.BlockSpec(memory_space=pltpu.SMEM)
HBM = pl.BlockSpec(memory_space=pltpu.HBM)


def row_slices(raster):
    return pl.pallas_call(
        slice_kernel,
        out_shape=(
            jax.ShapeDtypeStruct((FAR, COLS, CH), BF16),
            jax.ShapeDtypeStruct((NEAR, COLS, CH), BF16),
        ),
        in_specs=[HBM],
        out_specs=(VMEM, VMEM),
        scratch_shapes=[pltpu.SemaphoreType.DMA((2,))],
        name="row_slices",
    )(raster)


def first_layer(raster, above, below, conv1):
    return pl.pallas_call(
        first_kernel,
        out_shape=jax.ShapeDtypeStruct((2 * PAIRS_1, COLS, CH), BF16),
        in_specs=[VMEM] * 4,
        out_specs=VMEM,
        scratch_shapes=[
            pltpu.VMEM((NB1 + 1, COLS, 4 * CH), BF16),
            pltpu.VMEM((NB1 + 1, COLS, 4 * CH), BF16),
            pltpu.VMEM((2 * NB1 + 2, 80, CH), F32),
            pltpu.VMEM((12 * CH, 2 * CH), BF16),
        ],
        compiler_params=pltpu.CompilerParams(vmem_limit_bytes=32 * 2**20),
        cost_estimate=pl.CostEstimate(flops=4 * 10**9, bytes_accessed=5 * 10**6, transcendentals=0),
        name="first_layer",
    )(raster, above, below, conv1)


def scene(
    anchor, raster, above, below, left, right, inner, conv1, conv2, flags, gain, w_embed, w_qkv
):
    return pl.pallas_call(
        scene_kernel,
        out_shape=(
            jax.ShapeDtypeStruct((ROWS, COLS, CH), BF16),
            jax.ShapeDtypeStruct((128, 16, CH), BF16),
        ),
        in_specs=[SMEM] + [VMEM] * 12,
        out_specs=(HBM, VMEM),
        scratch_shapes=[
            pltpu.VMEM((2 * SLOTS * 64, CH), F32),
            pltpu.VMEM((NB1 + 1, STRIP, 6 * CH), BF16),
            pltpu.VMEM((NB1 + 1, STRIP, 6 * CH), BF16),
            pltpu.VMEM((2 * PAIRS_1, STRIP, CH), F32),
            pltpu.VMEM((2 * NB2 + 2, 96, CH), F32),
            pltpu.VMEM((NB2 + 1, WIDE, 6 * CH), BF16),
            pltpu.VMEM((NB2 + 1, WIDE, 6 * CH), BF16),
            pltpu.VMEM((2 * PAIRS_2 * WIDE, CH), F32),
            pltpu.VMEM((2 * PAIRS_2, COLS, CH), BF16),
            pltpu.VMEM((12 * CH, 2 * CH), BF16),
            pltpu.VMEM((12 * CH, 2 * CH), BF16),
            pltpu.VMEM((4, CROP, CH), F32),
            pltpu.VMEM((16 * 32, CH), F32),
            pltpu.SemaphoreType.DMA,
        ],
        compiler_params=pltpu.CompilerParams(vmem_limit_bytes=44 * 2**20),
        cost_estimate=pl.CostEstimate(flops=10**10, bytes_accessed=10**7, transcendentals=0),
        name="scene",
    )(
        anchor,
        raster,
        above,
        below,
        left,
        right,
        inner,
        conv1,
        conv2,
        flags,
        gain,
        w_embed,
        w_qkv,
    )


def attend(received):
    return pl.pallas_call(
        attend_kernel,
        out_shape=jax.ShapeDtypeStruct((128, 8, CH), BF16),
        in_specs=[VMEM],
        out_specs=VMEM,
        scratch_shapes=[pltpu.VMEM((1024, CH), F32), pltpu.VMEM((1024, CH), F32)],
        compiler_params=pltpu.CompilerParams(vmem_limit_bytes=24 * 2**20),
        cost_estimate=pl.CostEstimate(
            flops=10**10, bytes_accessed=10**6, transcendentals=2 * 10**6
        ),
        name="attend",
    )(received)


def finish(returned, live, gain, w_out, w_up, w_down):
    return pl.pallas_call(
        agent_kernel,
        out_shape=jax.ShapeDtypeStruct((32, 512), BF16),
        in_specs=[VMEM] * 5 + [HBM],
        out_specs=VMEM,
        scratch_shapes=[pltpu.VMEM(w_down.shape, BF16), pltpu.SemaphoreType.DMA],
        compiler_params=pltpu.CompilerParams(vmem_limit_bytes=50 * 2**20),
        name="agents",
    )(returned, live, gain, w_out, w_up, w_down)


def per_device(
    raster,
    conv_first,
    conv_second,
    crop_anchor,
    agent_live,
    w_embed,
    gain_attn,
    w_qkv,
    w_out,
    gain_mlp,
    w_up,
    w_down,
):
    def forward(n):
        return [(i, i + 1) for i in range(n - 1)]

    def backward(n):
        return [(i + 1, i) for i in range(n - 1)]

    def plain(x):
        return with_layout_constraint(x, Layout(major_to_minor=(0, 1, 2)))

    top, bottom = row_slices(raster)
    below = plain(lax.ppermute(top, "row", backward(8)))
    above = plain(lax.ppermute(bottom, "row", forward(8)))
    parts = (above, raster, below)
    last = jnp.concatenate([p[:, -NEAR:].transpose(1, 0, 2) for p in parts], axis=1)
    extra = jnp.concatenate([p[:, FAR - 1] for p in parts], axis=0)
    extra = jnp.pad(extra, ((0, 160 - KNOWN), (0, 0))).reshape(10, 16, CH)
    initial = jnp.concatenate([p[:, : FAR - 1] for p in parts] + [extra], axis=0)
    right = plain(lax.ppermute(plain(initial), "col", backward(16)))
    left = lax.ppermute(last, "col", forward(16))
    conv1 = conv_first.reshape(9, CH, CH)
    inner = first_layer(raster, above, below, conv1)
    flags = jnp.pad(agent_live.astype(F32)[None], ((0, 0), (96, 0)))
    features, payload = scene(
        crop_anchor,
        raster,
        above,
        below,
        left,
        right,
        inner,
        conv1,
        conv_second.reshape(9, CH, CH),
        flags,
        gain_attn[None],
        w_embed,
        w_qkv,
    )
    received = lax.all_to_all(payload, ("row", "col"), 0, 0, tiled=True)
    returned = lax.all_to_all(attend(received), ("row", "col"), 0, 0, tiled=True)
    live = agent_live.astype(F32)[:, None]
    agent_out = finish(returned, live, gain_mlp[None], w_out, w_up, w_down)
    return (features, agent_out)


def solution(mesh):
    in_specs = (
        P("row", "col", None),
        P(),
        P(),
        P(None, ("row", "col")),
        P(("row", "col")),
        P(),
        P(),
        P(),
        P(),
        P(),
        P(),
        P(),
    )
    out_specs = (P("row", "col", None), P(("row", "col"), None))
    return jax.shard_map(
        per_device, mesh=mesh, in_specs=in_specs, out_specs=out_specs, check_vma=False
    )
```

```python
import jax
import jax.numpy as jnp
from jax import lax
from jax.experimental import pallas as pl
from jax.experimental.pallas import tpu as pltpu
from jax.experimental.layout import Layout, with_layout_constraint
from jax.sharding import PartitionSpec as P

HEADS = 8
HEAD_DIM = 64
CROP = 16
EPS = 1e-06
SCORE_SCALE = 3.0

ROWS, COLS, CH = 128, 64, 128
NEAR, FAR = 2, 17
KNOWN = NEAR + ROWS + FAR
PAIRS_1 = 76
PAIRS_2 = 72
SLOTS = 77
NB1, NB2 = 19, 18
WIDE = 80
TOGETHER = 4
STRIP = 32
TAPS = ((0, 0), (0, 2), (1, 0), (1, 2), (0, 1), (1, 1))
F32, BF16 = jnp.float32, jnp.bfloat16


def dot(a, b):
    return lax.dot_general(a, b, (((1,), (0,)), ((), ())), preferred_element_type=F32)


def dot_t(a, b):
    return lax.dot_general(a, b, (((1,), (1,)), ((), ())), preferred_element_type=F32)


def iota(shape, dim):
    return lax.broadcasted_iota(jnp.int32, shape, dim)


def band(kernel_ref, band_ref):
    zero = jnp.zeros((CH, CH), BF16)
    for slot in range(2):
        for i, (par, b) in enumerate(TAPS):
            a = slot * 2 + par
            at = pl.ds((slot * 6 + i) * CH, CH)
            band_ref[at, 0:CH] = kernel_ref[a * 3 + b] if a < 3 else zero
            band_ref[at, CH : 2 * CH] = kernel_ref[(a - 1) * 3 + b] if a > 0 else zero


def rows_between(low, high, above_ref, raster_ref, below_ref):
    parts = []
    for ref, first, count in (
        (above_ref, 0, NEAR),
        (raster_ref, NEAR, ROWS),
        (below_ref, NEAR + ROWS, FAR),
    ):
        start, stop = max(low, first), min(high, first + count)
        if start < stop:
            parts.append(ref[start - first : stop - first])
    if high > KNOWN:
        parts.append(jnp.zeros((high - max(low, KNOWN), COLS, CH), BF16))
    return parts[0] if len(parts) == 1 else jnp.concatenate(parts, axis=0)


def row_inside(rho):
    return (rho >= 0) & (rho < ROWS * 8)


def slice_kernel(raster_hbm, top_ref, bottom_ref, sems):
    copies = [
        pltpu.make_async_copy(raster_hbm.at[pl.ds(0, FAR)], top_ref, sems.at[0]),
        pltpu.make_async_copy(raster_hbm.at[pl.ds(ROWS - NEAR, NEAR)], bottom_ref, sems.at[1]),
    ]
    for copy in copies:
        copy.start()
    for copy in copies:
        copy.wait()


def first_kernel(
    raster_ref,
    above_ref,
    below_ref,
    conv1_ref,
    inner_ref,
    shifted_a,
    shifted_b,
    row_wide,
    band_1,
):
    row_id = lax.axis_index("row")
    center = (above_ref, raster_ref, below_ref)
    band(conv1_ref, band_1)
    row_wide[:, 0:8] = jnp.zeros((2 * NB1 + 2, 8, CH), F32)
    row_wide[:, 72:80] = jnp.zeros((2 * NB1 + 2, 8, CH), F32)

    def spread(block, shifted):
        for i in range(NB1 + 1):
            for par in range(2):
                u = (block * NB1 + i) * 2 + par
                wide = row_wide.at[2 * i + par]
                wide[8:72] = rows_between(u, u + 1, *center)[0].astype(F32)
                shifted[i, :, (par * 2) * CH : (par * 2 + 1) * CH] = wide[7:71].astype(BF16)
                shifted[i, :, (par * 2 + 1) * CH : (par * 2 + 2) * CH] = wide[9:73].astype(BF16)

    def multiply(block, shifted):
        def side(s):
            u = (block * NB1 + s) * 2
            plain = rows_between(u, u + 2 * NB1, *center).reshape(NB1, 2, COLS, CH)
            parts = [shifted[s : s + NB1], plain[:, 0], plain[:, 1]]
            return jnp.concatenate(parts, axis=2).reshape(NB1 * COLS, 6 * CH)

        total = dot(side(0), band_1[0 : 6 * CH]) + dot(side(1), band_1[6 * CH :])
        total = jnp.maximum(total, 0.0)
        for i in range(NB1):
            for par in range(2):
                v = (block * NB1 + i) * 2 + par
                value = total[i * COLS : (i + 1) * COLS, par * CH : (par + 1) * CH]
                if v == 0 or v > ROWS:
                    value = jnp.where(row_inside(row_id * ROWS - 1 + v), value, 0.0)
                inner_ref[v] = value.astype(BF16)

    blocks = PAIRS_1 // NB1
    buffers = (shifted_a, shifted_b)
    spread(0, buffers[0])
    for block in range(blocks):
        multiply(block, buffers[block % 2])
        if block + 1 < blocks:
            spread(block + 1, buffers[(block + 1) % 2])


def scene_kernel(
    anchor_ref,
    raster_ref,
    above_ref,
    below_ref,
    left_ref,
    right_ref,
    inner_ref,
    conv1_ref,
    conv2_ref,
    flags_ref,
    gain_ref,
    w_embed,
    w_qkv,
    features_hbm,
    payload_ref,
    edge_wide,
    edge_a,
    edge_b,
    edge_first,
    row_first,
    shifted_a,
    shifted_b,
    wide_features,
    out_features,
    band_1,
    band_2,
    block_sum,
    pooled,
    out_sem,
):
    row_id = lax.axis_index("row")
    col_id = lax.axis_index("col")
    center = (above_ref, raster_ref, below_ref)
    band(conv1_ref, band_1)
    for u in range(2 * SLOTS):
        edge_wide[u * 64 + 48 : u * 64 + 56] = jnp.zeros((8, CH), F32)
    for c in range(NEAR):
        edge_wide[pl.ds(6 + c, KNOWN, stride=64)] = left_ref[c].astype(F32)
    last = right_ref[KNOWN : KNOWN + 10].reshape(160, CH).astype(F32)
    edge_wide[pl.ds(48, KNOWN, stride=64)] = last[:KNOWN]

    def edges(block, shifted):
        for i in range(NB1 + 1):
            for par in range(2):
                u = (block * NB1 + i) * 2 + par
                if u < KNOWN:
                    row = rows_between(u, u + 1, *center)[0]
                    edge_wide[u * 64 + 8 : u * 64 + 16] = row[0:16].astype(F32)[0:8]
                    edge_wide[u * 64 + 24 : u * 64 + 32] = row[48:64].astype(F32)[8:16]
                    edge_wide[u * 64 + 32 : u * 64 + 48] = right_ref[u].astype(F32)
                else:
                    edge_wide[u * 64 : u * 64 + 56] = jnp.zeros((56, CH), F32)
            for k, (par, b) in enumerate(TAPS):
                at = ((block * NB1 + i) * 2 + par) * 64 + b
                both = jnp.concatenate(
                    [edge_wide[at + 6 : at + 14], edge_wide[at + 30 : at + 54]], axis=0
                )
                shifted[i, :, k * CH : (k + 1) * CH] = both.astype(BF16)

    strip = iota((STRIP, CH), 0)
    column = col_id * COLS + jnp.where(strip < 8, strip - 1, strip + 55)
    column_in = (column >= 0) & (column < COLS * 16)

    def edge_multiply(block, shifted):
        def side(s):
            return shifted[s : s + NB1].reshape(NB1 * STRIP, 6 * CH)

        total = dot(side(0), band_1[0 : 6 * CH]) + dot(side(1), band_1[6 * CH :])
        total = jnp.maximum(total, 0.0)
        for i in range(NB1):
            for par in range(2):
                v = (block * NB1 + i) * 2 + par
                value = total[i * STRIP : (i + 1) * STRIP, par * CH : (par + 1) * CH]
                keep = column_in
                if v == 0 or v > ROWS:
                    keep = keep & row_inside(row_id * ROWS - 1 + v)
                edge_first[v] = jnp.where(keep, value, 0.0)

    def assemble(block, shifted):
        for i in range(NB2 + 1):
            for par in range(2):
                v = (block * NB2 + i) * 2 + par
                first = row_first.at[2 * i + par]
                first[8:72] = inner_ref[v].astype(F32)
                first[7:9] = edge_first[v, 0:2]
                first[71:95] = edge_first[v, 8:32]
            for k, (par, b) in enumerate(TAPS):
                window = row_first[2 * i + par, 7 + b : 7 + b + WIDE]
                shifted[i, :, k * CH : (k + 1) * CH] = window.astype(BF16)

    def multiply(block, shifted):
        def side(s):
            return shifted[s : s + NB2].reshape(NB2 * WIDE, 6 * CH)

        total = dot(side(0), band_2[0 : 6 * CH]) + dot(side(1), band_2[6 * CH :])
        for i in range(NB2):
            for par in range(2):
                row = (block * NB2 + i) * 2 + par
                u = row + NEAR
                middle = rows_between(u, u + 1, *center)[0].astype(F32)
                base = jnp.concatenate([middle, right_ref[u].astype(F32)], axis=0)
                value = total[i * WIDE : (i + 1) * WIDE, par * CH : (par + 1) * CH] + base
                value = value.astype(BF16)
                wide_features[row * WIDE : (row + 1) * WIDE] = value.astype(F32)
                out_features[row] = value[:COLS]

    blocks = PAIRS_1 // NB1
    buffers = (edge_a, edge_b)
    edges(0, buffers[0])
    for block in range(blocks):
        edge_multiply(block, buffers[block % 2])
        if block == 0:
            band(conv2_ref, band_2)
        if block + 1 < blocks:
            edges(block + 1, buffers[(block + 1) % 2])
    blocks = PAIRS_2 // NB2
    buffers = (shifted_a, shifted_b)
    assemble(0, buffers[0])
    for block in range(blocks):
        multiply(block, buffers[block % 2])
        if block + 1 < blocks:
            assemble(block + 1, buffers[(block + 1) % 2])
    out_copy = pltpu.make_async_copy(out_features.at[pl.ds(0, ROWS)], features_hbm, out_sem)
    out_copy.start()

    def crop(group, _):
        for sub in range(TOGETHER):
            agent = group * TOGETHER + sub
            top = anchor_ref[0, agent] - row_id * ROWS
            left = anchor_ref[1, agent] - col_id * COLS
            for rb in range(4):
                start = (top + rb * 4) * WIDE + left
                four = [wide_features[pl.ds(start + i * WIDE, CROP)] for i in range(4)]
                block_sum[sub * 4 + rb] = (four[0] + four[1]) + (four[2] + four[3])
        for sub in range(TOGETHER):
            agent = group * TOGETHER + sub
            for rb in range(4):
                cells = [block_sum[sub * 4 + rb, pl.ds(k, 4, stride=4)] for k in range(4)]
                mean = ((cells[0] + cells[1]) + (cells[2] + cells[3])) * (1.0 / 16)
                pooled[pl.ds(rb * 4 * 32 + agent, 4, stride=32)] = mean
        return _

    lax.fori_loop(0, 32 // TOGETHER, crop, 0)
    agents = jnp.concatenate(
        [pooled[b * 32 : (b + 1) * 32].astype(BF16) for b in range(16)], axis=1
    )
    embedded = dot(agents, w_embed[...])
    power = jnp.mean(embedded * embedded, axis=1, keepdims=True)
    normed = (embedded * lax.rsqrt(power + EPS) * gain_ref[...]).astype(BF16)
    projected = dot(normed, w_qkv[...])
    lane_id = iota((32, CH), 1)
    lower = lane_id < HEAD_DIM

    def unit(x):
        squared = x * x
        first_half = jnp.sum(jnp.where(lower, squared, 0.0), axis=1, keepdims=True)
        second_half = jnp.sum(jnp.where(lower, 0.0, squared), axis=1, keepdims=True)
        scale = lax.rsqrt(jnp.where(lower, first_half, second_half) * (1.0 / HEAD_DIM) + EPS)
        return x * scale

    def turned(x):
        return pltpu.roll(x, HEAD_DIM, 1)

    odd = lax.rem(lane_id // 16, 2) == 1
    flags = jnp.broadcast_to(flags_ref[...], (32, CH))
    flags = flags + pltpu.roll(flags, CH - 32, 1)
    extras = []
    for group in range(4):
        source = embedded[:, group * CH : (group + 1) * CH]
        high = source.astype(BF16).astype(F32)
        low = source - high
        low = jnp.where(odd, pltpu.roll(low, 16, 1), pltpu.roll(low, CH - 16, 1))
        extras.append(((turned(high), turned(low)), (high, low)))
    shift = lax.rem(col_id // 4, 4)
    for pair in range(4):
        q_two = unit(projected[:, pair * CH : (pair + 1) * CH])
        k_two = unit(projected[:, 512 + pair * CH : 512 + (pair + 1) * CH])
        v_two = projected[:, 1024 + pair * CH : 1024 + (pair + 1) * CH]
        rolled = (turned(q_two), turned(k_two), turned(v_two))
        for half in range(2):
            h = pair * 2 + half
            q_h = rolled[0] if half else q_two
            k_h = rolled[1] if half else k_two
            v_h = v_two if half else rolled[2]
            kv = jnp.where(lower, k_h, v_h)
            for kp in range(4):
                chunk = h * 4 + kp
                high, low = extras[chunk // 8][chunk % 8 // 4]
                place = lane_id // 16
                at = 4 + chunk % 4
                extra = jnp.where(place == at, high, jnp.where(place == at ^ 1, low, flags))
                row = jnp.where(lower, q_h, extra)
                for gg in range(4):
                    g = lax.rem(gg + shift, 4)
                    both = jnp.concatenate(
                        [kv[kp * 8 : kp * 8 + 8], row[gg * 8 : gg * 8 + 8]], axis=0
                    )
                    payload_ref[chunk * 4 + g] = both.astype(BF16)
    out_copy.wait()


def attend_kernel(received_ref, out_ref, queries, partial):
    device = lax.axis_index("row") * 16 + lax.axis_index("col")
    quarter = lax.rem(device // 4, 4)
    g = lax.rem(device, 4)
    everything = received_ref[...].astype(F32)
    kv = everything[:, 0:8].reshape(1024, CH)
    q_rows = everything[:, 8:16].reshape(1024, CH)
    queries[...] = q_rows
    flags = queries[pl.ds(0, 128, stride=8)].astype(BF16)
    key = iota((1024, CH), 0)
    lane = iota((1024, CH), 1)
    source = (key // 128) * 16 + quarter * 4 + lax.rem(key // 2, 4)
    chosen = dot((lane == source).astype(F32).astype(BF16), flags)
    first_flag = jnp.where(lax.rem(device // 4, 4) < 2, 96, 64)
    wanted = first_flag + lax.rem(key // 8, 16) * 2 + lax.rem(key, 2)
    alone = jnp.where(lane == wanted, chosen, 0.0).astype(BF16)
    mask = dot(alone, jnp.ones((CH, CH), BF16))
    lower = lane < HEAD_DIM
    keys = jnp.where(lower, kv, 0.0).astype(BF16)
    values = (jnp.where(lower, 1.0, kv) * mask).astype(BF16)
    factor = SCORE_SCALE / HEAD_DIM**0.5
    step = 256
    lane_s = iota((step, CH), 1)
    plain = (lane_s < first_flag) | (lane_s >= first_flag + 32)
    rounded = lane_s < first_flag + 16
    for i in range(1024 // step):
        q = queries[i * step : (i + 1) * step]
        weights = jnp.exp(dot_t(q.astype(BF16), keys) * factor).astype(BF16)
        summed = pltpu.roll(dot(weights, values), HEAD_DIM, 1)
        high = summed.astype(BF16).astype(F32)
        partial[i * step : (i + 1) * step] = jnp.where(
            lane_s < HEAD_DIM,
            summed,
            jnp.where(plain, q, jnp.where(rounded, high, summed - high)),
        )
    for r in range(8):
        for oh in range(4):
            dh = lax.rem(g - oh + 4, 4)
            for dl in range(4):
                base = (r * 4 + oh) * 32 + dl * 2
                rows = [partial[pl.ds(base + k, 4, stride=8)] for k in range(2)]
                out_ref[r * 16 + dh * 4 + dl] = jnp.concatenate(rows, axis=0).astype(BF16)


def agent_kernel(
    returned_ref, live_ref, gain_ref, w_out, w_up, w_down_hbm, out_ref, w_down, w_sem
):
    quarter = w_down.shape[0] // 4
    parts = [pl.ds(i * quarter, quarter) for i in range(4)]
    w_copies = [
        pltpu.make_async_copy(w_down_hbm.at[part], w_down.at[part], w_sem.at[i])
        for i, part in enumerate(parts)
    ]
    for w_copy in w_copies:
        w_copy.start()
    lane = iota((32, CH), 1)
    lower = lane < HEAD_DIM
    everything = returned_ref[...].astype(F32)
    attended = []
    embedded = []
    chunk_sum = None
    for h in range(HEADS):
        halves = [0.0, 0.0]
        for kp in range(4):
            chunk = h * 4 + kp
            block = everything[chunk * 4 : chunk * 4 + 4].reshape(32, CH)
            halves[kp // 2] += block
            placed = block + pltpu.roll(block, 16 if chunk % 2 else CH - 16, 1)
            if chunk % 8 < 4:
                placed = pltpu.roll(placed, HEAD_DIM, 1)
            here = (lane // 16) == chunk % 8
            chunk_sum = jnp.where(here, placed, 0.0 if chunk % 8 == 0 else chunk_sum)
            if chunk % 8 == 7:
                embedded.append(chunk_sum)
        parts = jnp.where((lane == 96) | (lane == 112), halves[0], 0.0)
        parts += jnp.where((lane == 64) | (lane == 80), halves[1], 0.0)
        ratio = (halves[0] + halves[1]) / jnp.sum(parts, axis=1, keepdims=True)
        if h % 2 == 0:
            even = ratio
        else:
            attended.append(jnp.where(lower, even, pltpu.roll(ratio, HEAD_DIM, 1)).astype(BF16))
    attended = jnp.concatenate(attended, axis=1)
    embedded = jnp.concatenate(embedded, axis=1)
    after = embedded + dot(attended, w_out[...])
    power = jnp.mean(after * after, axis=1, keepdims=True)
    normed = (after * lax.rsqrt(power + EPS) * gain_ref[...]).astype(BF16)
    activated = jax.nn.gelu(dot(normed, w_up[...])).astype(BF16)
    for w_copy in w_copies:
        w_copy.wait()
    result = (after + dot(activated, w_down[...])).astype(BF16)
    dh = lax.axis_index("col") // 4
    slot = iota((32, 32), 0)
    at = iota((32, 32), 1)
    g = lax.rem(slot // 8 + dh, 4)
    place = g * 8 + lax.rem(slot, 2) * 4 + lax.rem(slot // 2, 4)
    order = (at == place).astype(F32).astype(BF16)
    out_ref[...] = (dot(order, result) * live_ref[...]).astype(BF16)


VMEM = pl.BlockSpec(memory_space=pltpu.VMEM)
SMEM = pl.BlockSpec(memory_space=pltpu.SMEM)
HBM = pl.BlockSpec(memory_space=pltpu.HBM)


def row_slices(raster):
    return pl.pallas_call(
        slice_kernel,
        out_shape=(
            jax.ShapeDtypeStruct((FAR, COLS, CH), BF16),
            jax.ShapeDtypeStruct((NEAR, COLS, CH), BF16),
        ),
        in_specs=[HBM],
        out_specs=(VMEM, VMEM),
        scratch_shapes=[pltpu.SemaphoreType.DMA((2,))],
        name="row_slices",
    )(raster)


def first_layer(raster, above, below, conv1):
    return pl.pallas_call(
        first_kernel,
        out_shape=jax.ShapeDtypeStruct((2 * PAIRS_1, COLS, CH), BF16),
        in_specs=[VMEM] * 4,
        out_specs=VMEM,
        scratch_shapes=[
            pltpu.VMEM((NB1 + 1, COLS, 4 * CH), BF16),
            pltpu.VMEM((NB1 + 1, COLS, 4 * CH), BF16),
            pltpu.VMEM((2 * NB1 + 2, 80, CH), F32),
            pltpu.VMEM((12 * CH, 2 * CH), BF16),
        ],
        compiler_params=pltpu.CompilerParams(vmem_limit_bytes=32 * 2**20),
        cost_estimate=pl.CostEstimate(flops=4 * 10**9, bytes_accessed=5 * 10**6, transcendentals=0),
        name="first_layer",
    )(raster, above, below, conv1)


def scene(
    anchor, raster, above, below, left, right, inner, conv1, conv2, flags, gain, w_embed, w_qkv
):
    return pl.pallas_call(
        scene_kernel,
        out_shape=(
            jax.ShapeDtypeStruct((ROWS, COLS, CH), BF16),
            jax.ShapeDtypeStruct((128, 16, CH), BF16),
        ),
        in_specs=[SMEM] + [VMEM] * 12,
        out_specs=(HBM, VMEM),
        scratch_shapes=[
            pltpu.VMEM((2 * SLOTS * 64, CH), F32),
            pltpu.VMEM((NB1 + 1, STRIP, 6 * CH), BF16),
            pltpu.VMEM((NB1 + 1, STRIP, 6 * CH), BF16),
            pltpu.VMEM((2 * PAIRS_1, STRIP, CH), F32),
            pltpu.VMEM((2 * NB2 + 2, 96, CH), F32),
            pltpu.VMEM((NB2 + 1, WIDE, 6 * CH), BF16),
            pltpu.VMEM((NB2 + 1, WIDE, 6 * CH), BF16),
            pltpu.VMEM((2 * PAIRS_2 * WIDE, CH), F32),
            pltpu.VMEM((2 * PAIRS_2, COLS, CH), BF16),
            pltpu.VMEM((12 * CH, 2 * CH), BF16),
            pltpu.VMEM((12 * CH, 2 * CH), BF16),
            pltpu.VMEM((4 * TOGETHER, CROP, CH), F32),
            pltpu.VMEM((16 * 32, CH), F32),
            pltpu.SemaphoreType.DMA,
        ],
        compiler_params=pltpu.CompilerParams(vmem_limit_bytes=44 * 2**20),
        cost_estimate=pl.CostEstimate(flops=10**10, bytes_accessed=10**7, transcendentals=0),
        name="scene",
    )(
        anchor,
        raster,
        above,
        below,
        left,
        right,
        inner,
        conv1,
        conv2,
        flags,
        gain,
        w_embed,
        w_qkv,
    )


def attend(received):
    return pl.pallas_call(
        attend_kernel,
        out_shape=jax.ShapeDtypeStruct((128, 8, CH), BF16),
        in_specs=[VMEM],
        out_specs=VMEM,
        scratch_shapes=[pltpu.VMEM((1024, CH), F32), pltpu.VMEM((1024, CH), F32)],
        compiler_params=pltpu.CompilerParams(vmem_limit_bytes=24 * 2**20),
        cost_estimate=pl.CostEstimate(
            flops=10**10, bytes_accessed=10**6, transcendentals=2 * 10**6
        ),
        name="attend",
    )(received)


def finish(returned, live, gain, w_out, w_up, w_down):
    return pl.pallas_call(
        agent_kernel,
        out_shape=jax.ShapeDtypeStruct((32, 512), BF16),
        in_specs=[VMEM] * 5 + [HBM],
        out_specs=VMEM,
        scratch_shapes=[pltpu.VMEM(w_down.shape, BF16), pltpu.SemaphoreType.DMA((4,))],
        compiler_params=pltpu.CompilerParams(vmem_limit_bytes=50 * 2**20),
        name="agents",
    )(returned, live, gain, w_out, w_up, w_down)


def per_device(
    raster,
    conv_first,
    conv_second,
    crop_anchor,
    agent_live,
    w_embed,
    gain_attn,
    w_qkv,
    w_out,
    gain_mlp,
    w_up,
    w_down,
):
    def forward(n):
        return [(i, i + 1) for i in range(n - 1)]

    def backward(n):
        return [(i + 1, i) for i in range(n - 1)]

    def plain(x):
        return with_layout_constraint(x, Layout(major_to_minor=(0, 1, 2)))

    top, bottom = row_slices(raster)
    below = plain(lax.ppermute(top, "row", backward(8)))
    above = plain(lax.ppermute(bottom, "row", forward(8)))
    parts = (above, raster, below)
    last = jnp.concatenate([p[:, -NEAR:].transpose(1, 0, 2) for p in parts], axis=1)
    extra = jnp.concatenate([p[:, FAR - 1] for p in parts], axis=0)
    extra = jnp.pad(extra, ((0, 160 - KNOWN), (0, 0))).reshape(10, 16, CH)
    initial = jnp.concatenate([p[:, : FAR - 1] for p in parts] + [extra], axis=0)
    right = plain(lax.ppermute(plain(initial), "col", backward(16)))
    left = lax.ppermute(last, "col", forward(16))
    conv1 = conv_first.reshape(9, CH, CH)
    inner = first_layer(raster, above, below, conv1)
    flags = jnp.pad(agent_live.astype(F32)[None], ((0, 0), (96, 0)))
    features, payload = scene(
        crop_anchor,
        raster,
        above,
        below,
        left,
        right,
        inner,
        conv1,
        conv_second.reshape(9, CH, CH),
        flags,
        gain_attn[None],
        w_embed,
        w_qkv,
    )
    received = lax.all_to_all(payload, ("row", "col"), 0, 0, tiled=True)
    returned = lax.all_to_all(attend(received), ("row", "col"), 0, 0, tiled=True)
    live = agent_live.astype(F32)[:, None]
    agent_out = finish(returned, live, gain_mlp[None], w_out, w_up, w_down)
    return (features, agent_out)


def solution(mesh):
    in_specs = (
        P("row", "col", None),
        P(),
        P(),
        P(None, ("row", "col")),
        P(("row", "col")),
        P(),
        P(),
        P(),
        P(),
        P(),
        P(),
        P(),
    )
    out_specs = (P("row", "col", None), P(("row", "col"), None))
    return jax.shard_map(
        per_device, mesh=mesh, in_specs=in_specs, out_specs=out_specs, check_vma=False
    )
```

```python
import jax
import jax.numpy as jnp
from jax import lax
from jax.experimental import pallas as pl
from jax.experimental.pallas import tpu as pltpu
from jax.experimental.layout import Layout, with_layout_constraint
from jax.sharding import PartitionSpec as P

HEADS = 8
HEAD_DIM = 64
CROP = 16
EPS = 1e-06
SCORE_SCALE = 3.0

ROWS, COLS, CH = 128, 64, 128
NEAR, FAR = 2, 17
KNOWN = NEAR + ROWS + FAR
PAIRS_1 = 76
PAIRS_2 = 72
SLOTS = 77
NB1, NB2 = 19, 18
WIDE = 80
TOGETHER = 4
STRIP = 32
TAPS = ((0, 0), (0, 2), (1, 0), (1, 2), (0, 1), (1, 1))
F32, BF16 = jnp.float32, jnp.bfloat16


def dot(a, b):
    return lax.dot_general(a, b, (((1,), (0,)), ((), ())), preferred_element_type=F32)


def dot_t(a, b):
    return lax.dot_general(a, b, (((1,), (1,)), ((), ())), preferred_element_type=F32)


def iota(shape, dim):
    return lax.broadcasted_iota(jnp.int32, shape, dim)


def band(kernel_ref, band_ref):
    zero = jnp.zeros((CH, CH), BF16)
    for slot in range(2):
        for i, (par, b) in enumerate(TAPS):
            a = slot * 2 + par
            at = pl.ds((slot * 6 + i) * CH, CH)
            band_ref[at, 0:CH] = kernel_ref[a * 3 + b] if a < 3 else zero
            band_ref[at, CH : 2 * CH] = kernel_ref[(a - 1) * 3 + b] if a > 0 else zero


def rows_between(low, high, above_ref, raster_ref, below_ref):
    parts = []
    for ref, first, count in (
        (above_ref, 0, NEAR),
        (raster_ref, NEAR, ROWS),
        (below_ref, NEAR + ROWS, FAR),
    ):
        start, stop = max(low, first), min(high, first + count)
        if start < stop:
            parts.append(ref[start - first : stop - first])
    if high > KNOWN:
        parts.append(jnp.zeros((high - max(low, KNOWN), COLS, CH), BF16))
    return parts[0] if len(parts) == 1 else jnp.concatenate(parts, axis=0)


def row_inside(rho):
    return (rho >= 0) & (rho < ROWS * 8)


def slice_kernel(raster_hbm, top_ref, bottom_ref, sems):
    copies = [
        pltpu.make_async_copy(raster_hbm.at[pl.ds(0, FAR)], top_ref, sems.at[0]),
        pltpu.make_async_copy(raster_hbm.at[pl.ds(ROWS - NEAR, NEAR)], bottom_ref, sems.at[1]),
    ]
    for copy in copies:
        copy.start()
    for copy in copies:
        copy.wait()


def first_kernel(
    raster_ref,
    above_ref,
    below_ref,
    conv1_ref,
    inner_ref,
    shifted_a,
    shifted_b,
    row_wide,
    band_1,
):
    row_id = lax.axis_index("row")
    center = (above_ref, raster_ref, below_ref)
    band(conv1_ref, band_1)
    row_wide[:, 0:8] = jnp.zeros((2 * NB1 + 2, 8, CH), F32)
    row_wide[:, 72:80] = jnp.zeros((2 * NB1 + 2, 8, CH), F32)

    def spread(block, shifted):
        for i in range(NB1 + 1):
            for par in range(2):
                u = (block * NB1 + i) * 2 + par
                wide = row_wide.at[2 * i + par]
                wide[8:72] = rows_between(u, u + 1, *center)[0].astype(F32)
                shifted[i, :, (par * 2) * CH : (par * 2 + 1) * CH] = wide[7:71].astype(BF16)
                shifted[i, :, (par * 2 + 1) * CH : (par * 2 + 2) * CH] = wide[9:73].astype(BF16)

    def multiply(block, shifted):
        def side(s):
            u = (block * NB1 + s) * 2
            plain = rows_between(u, u + 2 * NB1, *center).reshape(NB1, 2, COLS, CH)
            parts = [shifted[s : s + NB1], plain[:, 0], plain[:, 1]]
            return jnp.concatenate(parts, axis=2).reshape(NB1 * COLS, 6 * CH)

        total = dot(side(0), band_1[0 : 6 * CH]) + dot(side(1), band_1[6 * CH :])
        total = jnp.maximum(total, 0.0)
        for i in range(NB1):
            for par in range(2):
                v = (block * NB1 + i) * 2 + par
                value = total[i * COLS : (i + 1) * COLS, par * CH : (par + 1) * CH]
                if v == 0 or v > ROWS:
                    value = jnp.where(row_inside(row_id * ROWS - 1 + v), value, 0.0)
                inner_ref[v] = value.astype(BF16)

    blocks = PAIRS_1 // NB1
    buffers = (shifted_a, shifted_b)
    spread(0, buffers[0])
    for block in range(blocks):
        multiply(block, buffers[block % 2])
        if block + 1 < blocks:
            spread(block + 1, buffers[(block + 1) % 2])


def scene_kernel(
    anchor_ref,
    raster_ref,
    above_ref,
    below_ref,
    left_ref,
    right_ref,
    inner_ref,
    conv1_ref,
    conv2_ref,
    flags_ref,
    gain_ref,
    w_embed,
    w_qkv,
    features_hbm,
    payload_ref,
    edge_wide,
    edge_a,
    edge_b,
    edge_first,
    row_first,
    shifted_a,
    shifted_b,
    wide_features,
    out_features,
    band_1,
    band_2,
    block_sum,
    pooled,
    out_sem,
):
    row_id = lax.axis_index("row")
    col_id = lax.axis_index("col")
    center = (above_ref, raster_ref, below_ref)
    band(conv1_ref, band_1)
    for u in range(2 * SLOTS):
        edge_wide[u * 64 + 48 : u * 64 + 56] = jnp.zeros((8, CH), F32)
    for c in range(NEAR):
        edge_wide[pl.ds(6 + c, KNOWN, stride=64)] = left_ref[c].astype(F32)
    last = right_ref[KNOWN : KNOWN + 10].reshape(160, CH).astype(F32)
    edge_wide[pl.ds(48, KNOWN, stride=64)] = last[:KNOWN]

    def edges(block, shifted):
        for i in range(NB1 + 1):
            for par in range(2):
                u = (block * NB1 + i) * 2 + par
                if u < KNOWN:
                    row = rows_between(u, u + 1, *center)[0]
                    edge_wide[u * 64 + 8 : u * 64 + 16] = row[0:16].astype(F32)[0:8]
                    edge_wide[u * 64 + 24 : u * 64 + 32] = row[48:64].astype(F32)[8:16]
                    edge_wide[u * 64 + 32 : u * 64 + 48] = right_ref[u].astype(F32)
                else:
                    edge_wide[u * 64 : u * 64 + 56] = jnp.zeros((56, CH), F32)
            for k, (par, b) in enumerate(TAPS):
                at = ((block * NB1 + i) * 2 + par) * 64 + b
                both = jnp.concatenate(
                    [edge_wide[at + 6 : at + 14], edge_wide[at + 30 : at + 54]], axis=0
                )
                shifted[i, :, k * CH : (k + 1) * CH] = both.astype(BF16)

    strip = iota((STRIP, CH), 0)
    column = col_id * COLS + jnp.where(strip < 8, strip - 1, strip + 55)
    column_in = (column >= 0) & (column < COLS * 16)

    def edge_multiply(block, shifted):
        def side(s):
            return shifted[s : s + NB1].reshape(NB1 * STRIP, 6 * CH)

        total = dot(side(0), band_1[0 : 6 * CH]) + dot(side(1), band_1[6 * CH :])
        total = jnp.maximum(total, 0.0)
        for i in range(NB1):
            for par in range(2):
                v = (block * NB1 + i) * 2 + par
                value = total[i * STRIP : (i + 1) * STRIP, par * CH : (par + 1) * CH]
                keep = column_in
                if v == 0 or v > ROWS:
                    keep = keep & row_inside(row_id * ROWS - 1 + v)
                edge_first[v] = jnp.where(keep, value, 0.0)

    def assemble(block, shifted):
        for i in range(NB2 + 1):
            for par in range(2):
                v = (block * NB2 + i) * 2 + par
                first = row_first.at[2 * i + par]
                first[8:72] = inner_ref[v].astype(F32)
                first[7:9] = edge_first[v, 0:2]
                first[71:95] = edge_first[v, 8:32]
            for k, (par, b) in enumerate(TAPS):
                window = row_first[2 * i + par, 7 + b : 7 + b + WIDE]
                shifted[i, :, k * CH : (k + 1) * CH] = window.astype(BF16)

    def multiply(block, shifted):
        def side(s):
            return shifted[s : s + NB2].reshape(NB2 * WIDE, 6 * CH)

        total = dot(side(0), band_2[0 : 6 * CH]) + dot(side(1), band_2[6 * CH :])
        for i in range(NB2):
            for par in range(2):
                row = (block * NB2 + i) * 2 + par
                u = row + NEAR
                middle = rows_between(u, u + 1, *center)[0].astype(F32)
                base = jnp.concatenate([middle, right_ref[u].astype(F32)], axis=0)
                value = total[i * WIDE : (i + 1) * WIDE, par * CH : (par + 1) * CH] + base
                value = value.astype(BF16)
                wide_features[row * WIDE : (row + 1) * WIDE] = value.astype(F32)
                out_features[row] = value[:COLS]

    blocks = PAIRS_1 // NB1
    buffers = (edge_a, edge_b)
    edges(0, buffers[0])
    for block in range(blocks):
        edge_multiply(block, buffers[block % 2])
        if block == 0:
            band(conv2_ref, band_2)
        if block + 1 < blocks:
            edges(block + 1, buffers[(block + 1) % 2])
    blocks = PAIRS_2 // NB2
    buffers = (shifted_a, shifted_b)
    assemble(0, buffers[0])
    for block in range(blocks):
        multiply(block, buffers[block % 2])
        if block + 1 < blocks:
            assemble(block + 1, buffers[(block + 1) % 2])
    out_copy = pltpu.make_async_copy(out_features.at[pl.ds(0, ROWS)], features_hbm, out_sem)
    out_copy.start()

    def crop(group, _):
        for sub in range(TOGETHER):
            agent = group * TOGETHER + sub
            top = anchor_ref[0, agent] - row_id * ROWS
            left = anchor_ref[1, agent] - col_id * COLS
            for rb in range(4):
                start = (top + rb * 4) * WIDE + left
                four = [wide_features[pl.ds(start + i * WIDE, CROP)] for i in range(4)]
                block_sum[sub * 4 + rb] = (four[0] + four[1]) + (four[2] + four[3])
        for sub in range(TOGETHER):
            agent = group * TOGETHER + sub
            for rb in range(4):
                cells = [block_sum[sub * 4 + rb, pl.ds(k, 4, stride=4)] for k in range(4)]
                mean = ((cells[0] + cells[1]) + (cells[2] + cells[3])) * (1.0 / 16)
                pooled[pl.ds(rb * 4 * 32 + agent, 4, stride=32)] = mean
        return _

    lax.fori_loop(0, 32 // TOGETHER, crop, 0)
    agents = jnp.concatenate(
        [pooled[b * 32 : (b + 1) * 32].astype(BF16) for b in range(16)], axis=1
    )
    embedded = dot(agents, w_embed[...])
    power = jnp.mean(embedded * embedded, axis=1, keepdims=True)
    normed = (embedded * lax.rsqrt(power + EPS) * gain_ref[...]).astype(BF16)
    projected = dot(normed, w_qkv[...])
    lane_id = iota((32, CH), 1)
    lower = lane_id < HEAD_DIM

    def unit(x):
        squared = x * x
        first_half = jnp.sum(jnp.where(lower, squared, 0.0), axis=1, keepdims=True)
        second_half = jnp.sum(jnp.where(lower, 0.0, squared), axis=1, keepdims=True)
        scale = lax.rsqrt(jnp.where(lower, first_half, second_half) * (1.0 / HEAD_DIM) + EPS)
        return x * scale

    def turned(x):
        return pltpu.roll(x, HEAD_DIM, 1)

    odd = lax.rem(lane_id // 16, 2) == 1
    flags = jnp.broadcast_to(flags_ref[...], (32, CH))
    flags = flags + pltpu.roll(flags, CH - 32, 1)
    extras = []
    for group in range(4):
        source = embedded[:, group * CH : (group + 1) * CH]
        high = source.astype(BF16).astype(F32)
        low = source - high
        low = jnp.where(odd, pltpu.roll(low, 16, 1), pltpu.roll(low, CH - 16, 1))
        extras.append(((turned(high), turned(low)), (high, low)))
    shift = lax.rem(col_id // 4, 4)
    for pair in range(4):
        q_two = unit(projected[:, pair * CH : (pair + 1) * CH])
        k_two = unit(projected[:, 512 + pair * CH : 512 + (pair + 1) * CH])
        v_two = projected[:, 1024 + pair * CH : 1024 + (pair + 1) * CH]
        rolled = (turned(q_two), turned(k_two), turned(v_two))
        for half in range(2):
            h = pair * 2 + half
            q_h = rolled[0] if half else q_two
            k_h = rolled[1] if half else k_two
            v_h = v_two if half else rolled[2]
            kv = jnp.where(lower, k_h, v_h)
            for kp in range(4):
                chunk = h * 4 + kp
                high, low = extras[chunk // 8][chunk % 8 // 4]
                place = lane_id // 16
                at = 4 + chunk % 4
                extra = jnp.where(place == at, high, jnp.where(place == at ^ 1, low, flags))
                row = jnp.where(lower, q_h, extra)
                for gg in range(4):
                    g = lax.rem(gg + shift, 4)
                    both = jnp.concatenate(
                        [kv[kp * 8 : kp * 8 + 8], row[gg * 8 : gg * 8 + 8]], axis=0
                    )
                    payload_ref[chunk * 4 + g] = both.astype(BF16)
    out_copy.wait()


def attend_kernel(received_ref, out_ref, queries, partial):
    device = lax.axis_index("row") * 16 + lax.axis_index("col")
    quarter = lax.rem(device // 4, 4)
    g = lax.rem(device, 4)
    everything = received_ref[...].astype(F32)
    kv = everything[:, 0:8].reshape(1024, CH)
    q_rows = everything[:, 8:16].reshape(1024, CH)
    queries[...] = q_rows
    flags = queries[pl.ds(0, 128, stride=8)].astype(BF16)
    key = iota((1024, CH), 0)
    lane = iota((1024, CH), 1)
    source = (key // 128) * 16 + quarter * 4 + lax.rem(key // 2, 4)
    chosen = dot((lane == source).astype(F32).astype(BF16), flags)
    first_flag = jnp.where(lax.rem(device // 4, 4) < 2, 96, 64)
    wanted = first_flag + lax.rem(key // 8, 16) * 2 + lax.rem(key, 2)
    alone = jnp.where(lane == wanted, chosen, 0.0).astype(BF16)
    mask = dot(alone, jnp.ones((CH, CH), BF16))
    lower = lane < HEAD_DIM
    keys = jnp.where(lower, kv, 0.0).astype(BF16)
    values = (jnp.where(lower, 1.0, kv) * mask).astype(BF16)
    factor = SCORE_SCALE / HEAD_DIM**0.5
    step = 256
    lane_s = iota((step, CH), 1)
    plain = (lane_s < first_flag) | (lane_s >= first_flag + 32)
    rounded = lane_s < first_flag + 16
    for i in range(1024 // step):
        q = queries[i * step : (i + 1) * step]
        weights = jnp.exp(dot_t(q.astype(BF16), keys) * factor).astype(BF16)
        summed = pltpu.roll(dot(weights, values), HEAD_DIM, 1)
        high = summed.astype(BF16).astype(F32)
        partial[i * step : (i + 1) * step] = jnp.where(
            lane_s < HEAD_DIM,
            summed,
            jnp.where(plain, q, jnp.where(rounded, high, summed - high)),
        )
    for r in range(8):
        for oh in range(4):
            dh = lax.rem(g - oh + 4, 4)
            for dl in range(4):
                base = (r * 4 + oh) * 32 + dl * 2
                rows = [partial[pl.ds(base + k, 4, stride=8)] for k in range(2)]
                out_ref[r * 16 + dh * 4 + dl] = jnp.concatenate(rows, axis=0).astype(BF16)


def agent_kernel(
    returned_ref, live_ref, gain_ref, w_out, w_up, w_down_hbm, out_ref, w_down, w_sem
):
    quarter = w_down.shape[0] // 4
    quarters = [pl.ds(i * quarter, quarter) for i in range(4)]
    w_copies = [
        pltpu.make_async_copy(w_down_hbm.at[part], w_down.at[part], w_sem.at[i])
        for i, part in enumerate(quarters)
    ]
    for w_copy in w_copies:
        w_copy.start()
    lane = iota((32, CH), 1)
    lower = lane < HEAD_DIM
    everything = returned_ref[...].astype(F32)
    attended = []
    embedded = []
    chunk_sum = None
    for h in range(HEADS):
        halves = [0.0, 0.0]
        for kp in range(4):
            chunk = h * 4 + kp
            block = everything[chunk * 4 : chunk * 4 + 4].reshape(32, CH)
            halves[kp // 2] += block
            placed = block + pltpu.roll(block, 16 if chunk % 2 else CH - 16, 1)
            if chunk % 8 < 4:
                placed = pltpu.roll(placed, HEAD_DIM, 1)
            here = (lane // 16) == chunk % 8
            chunk_sum = jnp.where(here, placed, 0.0 if chunk % 8 == 0 else chunk_sum)
            if chunk % 8 == 7:
                embedded.append(chunk_sum)
        parts = jnp.where((lane == 96) | (lane == 112), halves[0], 0.0)
        parts += jnp.where((lane == 64) | (lane == 80), halves[1], 0.0)
        ratio = (halves[0] + halves[1]) / jnp.sum(parts, axis=1, keepdims=True)
        if h % 2 == 0:
            even = ratio
        else:
            attended.append(jnp.where(lower, even, pltpu.roll(ratio, HEAD_DIM, 1)).astype(BF16))
    attended = jnp.concatenate(attended, axis=1)
    embedded = jnp.concatenate(embedded, axis=1)
    after = embedded + dot(attended, w_out[...])
    power = jnp.mean(after * after, axis=1, keepdims=True)
    normed = (after * lax.rsqrt(power + EPS) * gain_ref[...]).astype(BF16)
    activated = jax.nn.gelu(dot(normed, w_up[...])).astype(BF16)
    for i, w_copy in enumerate(w_copies):
        w_copy.wait()
        after = after + dot(activated[:, i * quarter : (i + 1) * quarter], w_down[quarters[i]])
    result = after.astype(BF16)
    dh = lax.axis_index("col") // 4
    slot = iota((32, 32), 0)
    at = iota((32, 32), 1)
    g = lax.rem(slot // 8 + dh, 4)
    place = g * 8 + lax.rem(slot, 2) * 4 + lax.rem(slot // 2, 4)
    order = (at == place).astype(F32).astype(BF16)
    out_ref[...] = (dot(order, result) * live_ref[...]).astype(BF16)


VMEM = pl.BlockSpec(memory_space=pltpu.VMEM)
SMEM = pl.BlockSpec(memory_space=pltpu.SMEM)
HBM = pl.BlockSpec(memory_space=pltpu.HBM)


def row_slices(raster):
    return pl.pallas_call(
        slice_kernel,
        out_shape=(
            jax.ShapeDtypeStruct((FAR, COLS, CH), BF16),
            jax.ShapeDtypeStruct((NEAR, COLS, CH), BF16),
        ),
        in_specs=[HBM],
        out_specs=(VMEM, VMEM),
        scratch_shapes=[pltpu.SemaphoreType.DMA((2,))],
        name="row_slices",
    )(raster)


def first_layer(raster, above, below, conv1):
    return pl.pallas_call(
        first_kernel,
        out_shape=jax.ShapeDtypeStruct((2 * PAIRS_1, COLS, CH), BF16),
        in_specs=[VMEM] * 4,
        out_specs=VMEM,
        scratch_shapes=[
            pltpu.VMEM((NB1 + 1, COLS, 4 * CH), BF16),
            pltpu.VMEM((NB1 + 1, COLS, 4 * CH), BF16),
            pltpu.VMEM((2 * NB1 + 2, 80, CH), F32),
            pltpu.VMEM((12 * CH, 2 * CH), BF16),
        ],
        compiler_params=pltpu.CompilerParams(vmem_limit_bytes=32 * 2**20),
        cost_estimate=pl.CostEstimate(flops=4 * 10**9, bytes_accessed=5 * 10**6, transcendentals=0),
        name="first_layer",
    )(raster, above, below, conv1)


def scene(
    anchor, raster, above, below, left, right, inner, conv1, conv2, flags, gain, w_embed, w_qkv
):
    return pl.pallas_call(
        scene_kernel,
        out_shape=(
            jax.ShapeDtypeStruct((ROWS, COLS, CH), BF16),
            jax.ShapeDtypeStruct((128, 16, CH), BF16),
        ),
        in_specs=[SMEM] + [VMEM] * 12,
        out_specs=(HBM, VMEM),
        scratch_shapes=[
            pltpu.VMEM((2 * SLOTS * 64, CH), F32),
            pltpu.VMEM((NB1 + 1, STRIP, 6 * CH), BF16),
            pltpu.VMEM((NB1 + 1, STRIP, 6 * CH), BF16),
            pltpu.VMEM((2 * PAIRS_1, STRIP, CH), F32),
            pltpu.VMEM((2 * NB2 + 2, 96, CH), F32),
            pltpu.VMEM((NB2 + 1, WIDE, 6 * CH), BF16),
            pltpu.VMEM((NB2 + 1, WIDE, 6 * CH), BF16),
            pltpu.VMEM((2 * PAIRS_2 * WIDE, CH), F32),
            pltpu.VMEM((2 * PAIRS_2, COLS, CH), BF16),
            pltpu.VMEM((12 * CH, 2 * CH), BF16),
            pltpu.VMEM((12 * CH, 2 * CH), BF16),
            pltpu.VMEM((4 * TOGETHER, CROP, CH), F32),
            pltpu.VMEM((16 * 32, CH), F32),
            pltpu.SemaphoreType.DMA,
        ],
        compiler_params=pltpu.CompilerParams(vmem_limit_bytes=44 * 2**20),
        cost_estimate=pl.CostEstimate(flops=10**10, bytes_accessed=10**7, transcendentals=0),
        name="scene",
    )(
        anchor,
        raster,
        above,
        below,
        left,
        right,
        inner,
        conv1,
        conv2,
        flags,
        gain,
        w_embed,
        w_qkv,
    )


def attend(received):
    return pl.pallas_call(
        attend_kernel,
        out_shape=jax.ShapeDtypeStruct((128, 8, CH), BF16),
        in_specs=[VMEM],
        out_specs=VMEM,
        scratch_shapes=[pltpu.VMEM((1024, CH), F32), pltpu.VMEM((1024, CH), F32)],
        compiler_params=pltpu.CompilerParams(vmem_limit_bytes=24 * 2**20),
        cost_estimate=pl.CostEstimate(
            flops=10**10, bytes_accessed=10**6, transcendentals=2 * 10**6
        ),
        name="attend",
    )(received)


def finish(returned, live, gain, w_out, w_up, w_down):
    return pl.pallas_call(
        agent_kernel,
        out_shape=jax.ShapeDtypeStruct((32, 512), BF16),
        in_specs=[VMEM] * 5 + [HBM],
        out_specs=VMEM,
        scratch_shapes=[pltpu.VMEM(w_down.shape, BF16), pltpu.SemaphoreType.DMA((4,))],
        compiler_params=pltpu.CompilerParams(vmem_limit_bytes=50 * 2**20),
        name="agents",
    )(returned, live, gain, w_out, w_up, w_down)


def per_device(
    raster,
    conv_first,
    conv_second,
    crop_anchor,
    agent_live,
    w_embed,
    gain_attn,
    w_qkv,
    w_out,
    gain_mlp,
    w_up,
    w_down,
):
    def forward(n):
        return [(i, i + 1) for i in range(n - 1)]

    def backward(n):
        return [(i + 1, i) for i in range(n - 1)]

    def plain(x):
        return with_layout_constraint(x, Layout(major_to_minor=(0, 1, 2)))

    top, bottom = row_slices(raster)
    below = plain(lax.ppermute(top, "row", backward(8)))
    above = plain(lax.ppermute(bottom, "row", forward(8)))
    parts = (above, raster, below)
    last = jnp.concatenate([p[:, -NEAR:].transpose(1, 0, 2) for p in parts], axis=1)
    extra = jnp.concatenate([p[:, FAR - 1] for p in parts], axis=0)
    extra = jnp.pad(extra, ((0, 160 - KNOWN), (0, 0))).reshape(10, 16, CH)
    initial = jnp.concatenate([p[:, : FAR - 1] for p in parts] + [extra], axis=0)
    right = plain(lax.ppermute(plain(initial), "col", backward(16)))
    left = lax.ppermute(last, "col", forward(16))
    conv1 = conv_first.reshape(9, CH, CH)
    inner = first_layer(raster, above, below, conv1)
    flags = jnp.pad(agent_live.astype(F32)[None], ((0, 0), (96, 0)))
    features, payload = scene(
        crop_anchor,
        raster,
        above,
        below,
        left,
        right,
        inner,
        conv1,
        conv_second.reshape(9, CH, CH),
        flags,
        gain_attn[None],
        w_embed,
        w_qkv,
    )
    received = lax.all_to_all(payload, ("row", "col"), 0, 0, tiled=True)
    returned = lax.all_to_all(attend(received), ("row", "col"), 0, 0, tiled=True)
    live = agent_live.astype(F32)[:, None]
    agent_out = finish(returned, live, gain_mlp[None], w_out, w_up, w_down)
    return (features, agent_out)


def solution(mesh):
    in_specs = (
        P("row", "col", None),
        P(),
        P(),
        P(None, ("row", "col")),
        P(("row", "col")),
        P(),
        P(),
        P(),
        P(),
        P(),
        P(),
        P(),
    )
    out_specs = (P("row", "col", None), P(("row", "col"), None))
    return jax.shard_map(
        per_device, mesh=mesh, in_specs=in_specs, out_specs=out_specs, check_vma=False
    )
```
